256 devices in a mesh: expert: 16 (over z, core), mp: 16 (over y, x).
Axes of the slice: x: 4, y: 4, z: 8, core: 2. Of those that a mesh axis runs over, the one named last changes fastest.
Arguments:
- tokens: bfloat16 [4096, 8192], P('expert', 'mp'), may hold values from -6 to 6
- queries: bfloat16 [4096, 8192], P('expert', 'mp'), may hold values from -6 to 6
- attn_keys: bfloat16 [4096, 8192], P('expert', 'mp'), may hold values from -6 to 6
- router: bfloat16 [8192, 2], P('mp'), may hold values from -0.0625 to 0.0625
- w_in: bfloat16 [8192, 65536], P(None, ('expert', 'mp')), may hold values from -0.0625 to 0.0625
- w_out: bfloat16 [65536, 8192], P(('expert', 'mp')), may hold values from -0.03125 to 0.03125
- pick_rows: int32 [2, 16, 16], P(None, 'expert'), may hold values from 0 to 255, as said below
- counts: int32 [2, 16], P(None, 'expert'), may hold values from 1 to 16, 128 in all within a row
Outputs:
- expert_mixed: bfloat16 [4096, 8192], P('expert', 'mp')
- attended: bfloat16 [4096, 8192], P('expert', 'mp')
The draws below stay inside these ranges and needn't reach their ends.
Inputs may be any that keep to these rules, and one draw needn't show every extreme that they name: `pick_rows`: for each expert and source block the 16 entries are distinct rows of that block; only the first counts entries are picks. `counts`: each expert picks 128 tokens in all.
All inputs are finite; a program needn't handle non-finite values. No bound on the sum of `counts` on one device may be relied on, other than what follows from the above.
Results may differ from the reference program's by a relative error of at most 0.0059.
Values may be sent and summed in bfloat16 or wider, within the bound.
A program may use at most 128 MiB of HBM per device.

```python
import math
import jax
import jax.numpy as jnp
import numpy as np
from jax import lax

D = 8192
HEADS = 64
HEAD_DIM = 128
FF = 32768
EXPERTS = 2
TOK_DEV = 256
TOKENS = 4096
SLOT = 16
CAP = 128
N_EXPERT = 16


def draw_queries(key, part):
    key = jax.random.fold_in(key, 5)
    return jnp.clip(jax.random.normal(key, (TOKENS, D), jnp.float32), -6.0, 6.0).astype(jnp.bfloat16)


def draw_attn_keys(key, part):
    key = jax.random.fold_in(key, 7)
    return jnp.clip(jax.random.normal(key, (TOKENS, D), jnp.float32), -6.0, 6.0).astype(jnp.bfloat16)


def draw_pick_rows(key, part):
    key = jax.random.fold_in(key, 3)
    subkeys = jax.random.split(key, EXPERTS * N_EXPERT)
    chosen = jax.vmap(lambda subkey: jax.random.permutation(subkey, TOK_DEV)[:SLOT])(subkeys)
    return chosen.reshape(EXPERTS, N_EXPERT, SLOT).astype(jnp.int32)


def level_of(rng, dims, pieces, low, top_value):
    def one(dim, blocks):
        draws = jax.random.uniform(jax.random.fold_in(jax.random.fold_in(rng, 6), dim), (blocks,), jnp.float32, low / len(pieces), top_value / len(pieces))
        return jnp.repeat(jnp.exp(draws), dims[dim] // blocks).reshape((-1,) + (1,) * (len(dims) - dim - 1))

    factor_of = one(*pieces[0])
    for cut in pieces[1:]:
        factor_of = factor_of * one(*cut)
    return factor_of


def profile(count, total, limit, skew):
    portions = [(1 << 20) // math.isqrt(grade ** skew) + 1 for grade in range(2, count + 1)]
    spare, holding = total - limit - (count - 1), [1] * (count - 1)
    while spare > 0:
        movable = [i for i in range(count - 1) if holding[i] < limit]
        mass, budget = sum([portions[i] for i in movable]), spare
        for i in movable:
            addition = min(limit - holding[i], max(1, budget * portions[i] // mass), spare)
            holding[i] = holding[i] + addition
            spare = spare - addition
    return np.array([limit] + holding)


def ragged(rng, count, total, limit, slope):
    if count == 2:
        one = jax.random.randint(rng, (), max(1, total - limit), min(limit, total - 1) + 1)
        return jnp.stack([one, total - one])
    sizes = jnp.asarray(profile(count, total, limit, slope), jnp.int32)
    twos = (count - 1) // 2
    giver, sink = sizes[1:1 + 2 * twos:2], sizes[2:2 + 2 * twos:2]
    slack = jnp.minimum(giver - 1, limit - sink)
    passed = jax.random.randint(jax.random.fold_in(rng, 1), (twos,), 0, 1 << 20) % (slack + 1)
    sizes = sizes.at[1:1 + 2 * twos:2].set(giver - passed).at[2:2 + 2 * twos:2].set(sink + passed)
    return sizes[jax.random.permutation(jax.random.fold_in(rng, 2), count)]


def normal_values(stream_key, extent, spread, most, cuts=(), kind=jnp.bfloat16):
    factor_of = level_of(stream_key, extent, cuts, -0.22, 0.18) if cuts else 1.0
    values = jax.random.normal(stream_key, extent, jnp.float32) * spread * factor_of
    return jnp.minimum(jnp.maximum(values, -most), most).astype(kind)


def setup_inputs(seed: int = 0) -> dict:
    streams_of = jax.random.split(jax.random.key(seed), 9)
    tokens = normal_values(streams_of[0], (TOKENS, D), 1.0, 6.0, ((0, 16), (1, 16)))
    queries = draw_queries(jax.random.fold_in(streams_of[8], 71), 0)
    attn_keys = draw_attn_keys(jax.random.fold_in(streams_of[8], 71), 0)
    router = normal_values(streams_of[3], (D, EXPERTS), D ** -0.5, 0.0625, ((0, 16),))
    w_in = normal_values(streams_of[4], (D, EXPERTS * FF), D ** -0.5, 0.0625, ((1, 256),))
    w_out = normal_values(streams_of[5], (EXPERTS * FF, D), FF ** -0.5, 0.03125, ((0, 256),))
    pick_rows = draw_pick_rows(jax.random.fold_in(streams_of[8], 71), 0)
    counts = jax.vmap(lambda own: ragged(own, N_EXPERT, CAP, SLOT, 2))(jax.random.split(streams_of[7], EXPERTS)).reshape((EXPERTS, N_EXPERT)).astype(jnp.int32)
    return {"tokens": tokens, "queries": queries, "attn_keys": attn_keys, "router": router, "w_in": w_in, "w_out": w_out, "pick_rows": pick_rows, "counts": counts}


def reference(tokens, queries, attn_keys, router, w_in, w_out, pick_rows, counts):
    logits = jnp.dot(tokens, router, preferred_element_type=jnp.float32)
    update = jnp.zeros((TOKENS, D), jnp.float32)
    offsets = (jnp.arange(N_EXPERT, dtype=jnp.int32) * TOK_DEV)[:, None]
    for expert in range(EXPERTS):
        row_index = (offsets + pick_rows[expert].astype(jnp.int32)).reshape(-1)
        live_slots = (jnp.arange(SLOT, dtype=jnp.int32)[None, :] < counts[expert][:, None]).reshape(-1)
        picked_rows = jnp.where(live_slots[:, None], tokens[row_index], 0).astype(jnp.bfloat16)
        preact = jnp.dot(picked_rows, w_in[:, expert * FF:(expert + 1) * FF], preferred_element_type=jnp.float32)
        hidden = jax.nn.gelu(preact).astype(jnp.bfloat16)
        out_rows = jnp.dot(hidden, w_out[expert * FF:(expert + 1) * FF], preferred_element_type=jnp.float32)
        gate_value = jnp.where(live_slots, jax.nn.sigmoid(logits[row_index, expert]), 0.0)
        update = update.at[row_index].add(gate_value[:, None] * out_rows)
    expert_mixed = (tokens.astype(jnp.float32) + update).astype(jnp.bfloat16)

    positions = jnp.arange(TOKENS, dtype=jnp.int32)
    allowed = positions[None, :] <= positions[:, None]
    inv_root = HEAD_DIM ** -0.5

    def head_attention(operands):
        query_head, key_head, value_head = operands
        scores = jnp.dot(query_head, key_head.T, preferred_element_type=jnp.float32) * inv_root
        masked = jnp.where(allowed, scores, -1e30)
        top_score = jnp.max(masked, axis=1, keepdims=True)
        weights = jnp.where(allowed, jnp.exp(scores - top_score), 0.0)
        denominator = jnp.sum(weights, axis=1, keepdims=True)
        numerator = jnp.dot(weights.astype(jnp.bfloat16), value_head, preferred_element_type=jnp.float32)
        return numerator / denominator

    query_heads = queries.reshape(TOKENS, HEADS, HEAD_DIM).transpose(1, 0, 2)
    key_heads = attn_keys.reshape(TOKENS, HEADS, HEAD_DIM).transpose(1, 0, 2)
    value_heads = expert_mixed.reshape(TOKENS, HEADS, HEAD_DIM).transpose(1, 0, 2)
    results = lax.map(head_attention, (query_heads, key_heads, value_heads))
    attended = results.transpose(1, 0, 2).reshape(TOKENS, D).astype(jnp.bfloat16)
    return expert_mixed, attended
```

```python
import jax
import jax.numpy as jnp
from jax import lax
from jax.experimental import pallas as pl
from jax.experimental.pallas import tpu as pltpu
from jax.sharding import PartitionSpec as P

MESH = pl.DeviceIdType.MESH
HEAD_DIM = 128
BF = jnp.bfloat16
F32 = jnp.float32
NT = (((1,), (1,)), ((), ()))
INV_ROOT = HEAD_DIM ** (-0.5)
CUT, BLOCK_ROWS = 80, 144


def dot(a, b):
    return jnp.dot(a, b, preferred_element_type=F32)


def dot_nt(a, b):
    return lax.dot_general(a, b, NT, preferred_element_type=F32)


def kernel(
    tok, qry, key, rt, win, wout, picks, cnts, mixed_o, att_o,
    a_msg, a_buf, xg, w1, w2, part, part_in, lgacc, hid, gate_s,
    outb, t_own, rs_h, rs_f, t_sum, rp_h, rp_f, e_buf, u_buf,
    kb, vb, acc, mrow, lrow, kp, wp, pos_col, pos_row,
    loc_sem, a_ss, a_rs, w_ss, w_rs, g_ss, g_rs, x_ss, x_rs,
    r_ss, r_rs, e_ss, e_rs, ep_ss, ep_rs, kv_ss, kv_rs, kvp_ss, kvp_rs,
):
    e = lax.axis_index("expert")
    m = lax.axis_index("mp")
    z, c = e // 2, lax.rem(e, 2)
    y, x = m // 4, lax.rem(m, 4)
    oc = 1 - c
    group = z // 4

    def dev(dz=0, dc=0, dy=0, dx=0):
        zz = lax.rem(z + dz + 8, 8)
        cc = lax.rem(c + dc, 2)
        return (zz * 2 + cc, lax.rem(y + dy + 4, 4) * 4 + lax.rem(x + dx + 4, 4))

    def along(i, j):
        return c * i + oc * j, oc * i + c * j

    def blk(i, j):
        dy, dx = along(i, j)
        return lax.rem(y + dy + 4, 4) * 4 + lax.rem(x + dx + 4, 4)

    def pdev(d):
        dy, dx = along(d, 0)
        return dev(dy=dy, dx=dx)

    def sdev(d):
        dy, dx = along(0, d)
        return dev(dy=dy, dx=dx)

    partner = dev(dc=1)
    sent = []

    def send(src, dst, ss, rs, to):
        cp = pltpu.make_async_remote_copy(
            src_ref=src, dst_ref=dst, send_sem=ss, recv_sem=rs, device_id=to, device_id_type=MESH
        )
        cp.start()
        sent.append(cp)
        return cp

    w1_loc = pltpu.make_async_copy(win.at[:, c], w1.at[c], loc_sem.at[0])
    w1_loc.start()
    barrier = pltpu.get_barrier_semaphore()
    for dz in range(8):
        for dc in range(2):
            if dz or dc:
                pl.semaphore_signal(barrier, inc=1, device_id=dev(dz, dc), device_id_type=MESH)
    for d in (1, -1):
        pl.semaphore_signal(barrier, inc=1, device_id=dev(dy=d), device_id_type=MESH)
        pl.semaphore_signal(barrier, inc=1, device_id=dev(dx=d), device_id_type=MESH)

    row32 = lax.broadcasted_iota(jnp.int32, (32, 256), 0)
    lane32 = lax.broadcasted_iota(jnp.int32, (32, 256), 1)
    chosen = jnp.full((32, 256), -1, jnp.int32)
    row16 = lax.broadcasted_iota(jnp.int32, (16, 128), 0)
    lane16 = lax.broadcasted_iota(jnp.int32, (16, 128), 1)
    meta = jnp.where(row16 == 0, cnts[0, 0], jnp.where(row16 == 1, cnts[1, 0], 0))
    base = 16 * lax.rem(e, 8)
    for g in range(2):
        for j in range(16):
            pick = picks[g, 0, j]
            live = jnp.where(j < cnts[g, 0], pick, -1)
            chosen = jnp.where(row32 == 16 * g + j, live, chosen)
            meta = jnp.where(
                (row16 == 2 + 2 * g + e // 8) & (lane16 == base + j), pick, meta
            )
    onehot = jnp.where(chosen == lane32, 1.0, 0.0).astype(BF)
    rows = dot(onehot, tok[...]).astype(BF)
    meta_b = meta.astype(F32).astype(BF)
    for g in range(2):
        for h in range(2):
            a_msg[g, h, 0:16, :] = rows[16 * g : 16 * g + 16, 256 * h : 256 * h + 128]
            a_msg[g, h, 16:32, :] = rows[16 * g : 16 * g + 16, 256 * h + 128 : 256 * h + 256]
            a_msg[g, h, 32:48, :] = meta_b
    a_buf[e] = a_msg[group, c]
    pl.semaphore_wait(barrier, 19)

    a_cps = []
    for dz in (4, 3, 5, 2, 6, 1, 7, 0):
        for dc in range(2):
            if dz or dc:
                to_plane = lax.rem(z + dz, 8)
                to_core = lax.rem(c + dc, 2)
                a_cps.append(
                    send(
                        a_msg.at[to_plane // 4, to_core], a_buf.at[e],
                        a_ss.at[dz * 2 + dc], a_rs.at[dz * 2 + dc], dev(dz, dc),
                    )
                )

    def kv_send(buf, which, r_from, r_to, way, src=None):
        src = buf.at[r_from, c] if src is None else src
        return send(
            src, buf.at[r_to, c], kv_ss.at[which, r_to, way], kv_rs.at[which, r_to, way],
            dev(dz=1 if way == 0 else -1),
        )

    def kv_share(buf, which, r, src=None):
        src = buf.at[r, c] if src is None else src
        return send(src, buf.at[r, c], kvp_ss.at[which, r], kvp_rs.at[which, r], partner)

    pieces = {}
    shared = {}
    pieces["k", 1] = kv_send(kb, 0, 0, 1, 0, key)
    pieces["v", 7] = kv_send(vb, 1, 0, 7, 1, tok)
    shared["k", 0] = kv_share(kb, 0, 0, key)
    shared["v", 0] = kv_share(vb, 1, 0, tok)
    pieces["v", 1] = kv_send(vb, 1, 0, 1, 0, tok)
    pieces["k", 7] = kv_send(kb, 0, 0, 7, 1, key)
    right = [("k", 1), ("v", 1), ("k", 2), ("v", 2), ("k", 3), ("v", 3), ("k", 4)]
    left = [("v", 7), ("k", 7), ("v", 6), ("k", 6), ("v", 5), ("k", 5), ("v", 4)]

    def pump(n):
        for way, (what, r) in ((0, right[n]), (1, left[n])):
            pieces[what, r].wait_recv()
            which, buf = (0, kb) if what == "k" else (1, vb)
            r_to = r + 1 if way == 0 else r - 1
            if (what, r_to) in (right if way == 0 else left):
                pieces[what, r_to] = kv_send(buf, which, r, r_to, way)
            shared[what, r] = kv_share(buf, which, r)

    w1_far = send(win.at[:, oc], w1.at[c], w_ss.at[0], w_rs.at[0], partner)

    def w2_copies():
        for b in range(16):
            mine = pl.ds(pl.multiple_of(512 * b + 256 * c, 256), 256)
            pltpu.make_async_copy(wout.at[:, mine], w2.at[c, b], loc_sem.at[1]).start()
        for b in range(16):
            other = pl.ds(pl.multiple_of(512 * b + 256 * oc, 256), 256)
            pltpu.make_async_remote_copy(
                src_ref=wout.at[:, other], dst_ref=w2.at[c, b], send_sem=w_ss.at[1],
                recv_sem=w_rs.at[1], device_id=partner, device_id_type=MESH,
            ).start()

    w2_copies()
    w2_loc = pltpu.make_async_copy(w2.at[c], w2.at[c], loc_sem.at[1])
    w2_far = pltpu.make_async_remote_copy(
        src_ref=w2.at[c], dst_ref=w2.at[c], send_sem=w_ss.at[1], recv_sem=w_rs.at[1],
        device_id=partner, device_id_type=MESH,
    )

    def soft_step(h, scores, v_h):
        hs = pl.ds(pl.multiple_of(h * 128, 128), 128)
        old = mrow[h][:, 0:1]
        new = jnp.maximum(old, jnp.max(scores, axis=1, keepdims=True))
        alpha = jnp.exp((old - new) * INV_ROOT)
        w = jnp.exp((scores - new) * INV_ROOT)
        total = w[:, 0:128]
        for i in range(1, scores.shape[1] // 128):
            total = total + w[:, 128 * i : 128 * i + 128]
        lrow[h] = lrow[h] * alpha + total
        acc[:, hs] = acc[:, hs] * alpha + dot(w.astype(BF), v_h)
        mrow[h] = jnp.broadcast_to(new, (256, 128))

    def attend_own():
        allowed = lax.broadcasted_iota(jnp.int32, (256, 256), 1) <= lax.broadcasted_iota(
            jnp.int32, (256, 256), 0
        )

        @pl.loop(0, 4)
        def _(h):
            hs = pl.ds(pl.multiple_of(h * 128, 128), 128)
            scores = jnp.where(allowed, dot_nt(qry[:, hs], key[:, hs]), -1e30)
            new = jnp.max(scores, axis=1, keepdims=True)
            w = jnp.exp((scores - new) * INV_ROOT)
            lrow[h] = w[:, 0:128] + w[:, 128:256]
            acc[:, hs] = dot(w.astype(BF), tok[:, hs])
            mrow[h] = jnp.broadcast_to(new, (256, 128))

    def attend_partner():
        @pl.loop(0, 4)
        def _(h):
            hs = pl.ds(pl.multiple_of(h * 128, 128), 128)
            soft_step(h, dot_nt(qry[:, hs], kb[0, 0, :, hs]), vb[0, 0, :, hs])

    def attend_chip(r):
        @pl.loop(0, 4)
        def _(h):
            hs = pl.ds(pl.multiple_of(h * 128, 128), 128)
            k_h = kb[r, :, :, hs].reshape(512, 128)
            v_h = vb[r, :, :, hs].reshape(512, 128)
            soft_step(h, dot_nt(qry[:, hs], k_h), v_h)

    def pick_keys(first, k_rows):
        n = k_rows.shape[0]
        at = lax.broadcasted_iota(jnp.int32, (256, n), 1) + first
        sel = jnp.where(pos_col[:, 0:1] == at, 1.0, 0.0).astype(BF)
        kp[...] += dot(sel, k_rows)

    def attend_far(d):
        for r, ok in ((d, z >= d), (8 - d, z >= 8 - d)):
            for what in ("k", "v"):
                shared[what, r].wait_recv()

            @pl.when(ok)
            def _():
                attend_chip(r)
                pick_keys((z - r) * 512, kb[r].reshape(512, 512))

            if d == 4:
                break

    attend_own()
    for what in ("k", "v"):
        shared[what, 0].wait_recv()

    @pl.when(c == 1)
    def _():
        attend_partner()

    for cp in a_cps:
        cp.wait_recv()
    lane_f = lane16.astype(F32)
    run = jnp.zeros((16, 128), F32)
    slot_at = [jnp.full((16, 128), -1.0, F32), jnp.full((16, 128), -1.0, F32)]
    picked_lane = jnp.zeros((16, 128), F32)
    for s in range(16):
        t = a_buf[s, 32:48, :].astype(F32)
        j = lane_f - 16.0 * (s % 8)
        here = (lane16 // 16 == s % 8) & (j < t)
        slot_at[s // 8] = jnp.where(here, run + j, slot_at[s // 8])
        run = run + t
        picked_lane = picked_lane + t
    row_f = lax.broadcasted_iota(jnp.int32, (128, 256), 0).astype(F32)
    row_l = lax.broadcasted_iota(jnp.int32, (16, 256), 0)
    lane_l = lax.broadcasted_iota(jnp.int32, (16, 256), 1)
    compact = []
    for g in range(2):
        at = jnp.concatenate([slot_at[0][g : g + 1], slot_at[1][g : g + 1]], axis=1)
        cmat = jnp.where(row_f == at, 1.0, 0.0).astype(BF)
        compact.append(cmat)
    mine = jnp.where(group == 0, compact[0].astype(F32), compact[1].astype(F32)).astype(BF)
    for h in range(2):
        got = a_buf[:, 16 * h : 16 * h + 16, :].reshape(256, 128)
        xg[m, 0:128, 128 * h : 128 * h + 128] = dot(mine, got).astype(BF)
    half_lanes = pl.ds(pl.multiple_of(256 * c, 256), 256)
    xg[m, 128:144, :] = rt[group, :, half_lanes]

    g_cps = {}

    def g_send(idx, b, lo, hi, to):
        g_cps[idx] = send(
            xg.at[b, pl.ds(lo, hi - lo)], xg.at[b, pl.ds(lo, hi - lo)],
            g_ss.at[idx], g_rs.at[idx], to,
        )

    def g_second(i):
        g_send(4 + 4 * i, blk(i, 0), 0, BLOCK_ROWS, sdev(1))
        g_send(5 + 4 * i, blk(i, 0), 0, BLOCK_ROWS, sdev(-1))

    def g_second_half(i):
        g_cps[4 + 4 * i].wait_recv()
        g_send(6 + 4 * i, blk(i, 3), 0, CUT, sdev(1))
        g_cps[5 + 4 * i].wait_recv()
        g_send(7 + 4 * i, blk(i, 1), CUT, BLOCK_ROWS, sdev(-1))

    g_send(0, m, 0, BLOCK_ROWS, pdev(1))
    g_send(1, m, 0, BLOCK_ROWS, pdev(-1))
    g_second(0)

    at_lane = []
    for g in range(2):
        pk = jnp.concatenate(
            [picked_lane[2 + 2 * g : 3 + 2 * g], picked_lane[3 + 2 * g : 4 + 2 * g]], axis=1
        )
        info = jnp.where(
            row_l == 0, jnp.broadcast_to(pk, (16, 256)), (lane_l // 16).astype(F32)
        ).astype(BF)
        col = dot_nt(compact[g], info)
        pos_col[128 * g : 128 * g + 128, :] = jnp.broadcast_to(
            (col[:, 0:1] + 256.0 * col[:, 1:2]).astype(jnp.int32), (128, 128)
        )
        lane = dot_nt(info, compact[g])
        at_lane.append((lane[0:1] + 256.0 * lane[1:2]).astype(jnp.int32))
    pos_row[...] = jnp.broadcast_to(jnp.concatenate(at_lane, axis=1), (8, 256))
    kp[...] = jnp.zeros((256, 512), F32)
    pick_keys(e * 256, key[...])

    @pl.when(c == 1)
    def _():
        pick_keys(z * 512, kb[0, 0])

    pump(0)
    part[...] = jnp.zeros((128, 640), F32)
    lgacc[...] = jnp.zeros((128, 16), F32)
    w1_loc.wait()
    w1_far.wait_recv()

    def mm1(i, j):
        b = blk(i, j)
        xb = xg[b, 0:128, :]
        part[:, 0:256] += dot(xb, w1[0, b])
        part[:, 256:512] += dot(xb, w1[1, b])
        lgacc[...] += dot_nt(xb, xg[b, 128:144, :])

    mm1(0, 0)
    g_cps[0].wait_recv()
    g_send(2, blk(3, 0), 0, CUT, pdev(1))
    g_second(3)
    g_cps[1].wait_recv()
    g_send(3, blk(1, 0), CUT, BLOCK_ROWS, pdev(-1))
    g_second(1)
    mm1(3, 0)
    mm1(1, 0)
    g_second_half(0)
    mm1(0, 3)
    mm1(0, 1)
    g_cps[2].wait_recv()
    g_cps[3].wait_recv()
    g_second(2)
    mm1(2, 0)
    pump(1)
    for i in (3, 1, 2):
        g_second_half(i)
        mm1(i, 3)
        mm1(i, 1)
    attend_far(1)
    pump(2)
    for i in (0, 3, 1, 2):
        g_cps[6 + 4 * i].wait_recv()
        g_cps[7 + 4 * i].wait_recv()
        mm1(i, 2)

    part[:, 512:640] = jnp.broadcast_to(lgacc[:, 0:1], (128, 128))
    x_cp = send(part, part_in, x_ss.at[0], x_rs.at[0], partner)
    w2_loc.wait()
    w2_far.wait_recv()
    x_cp.wait_recv()
    hid[...] = jax.nn.gelu(part[:, 0:512] + part_in[:, 0:512]).astype(BF)
    gate_s[...] = jax.nn.sigmoid(part[:, 512:640] + part_in[:, 512:640])

    def mm2(i, j):
        b = blk(i, j)
        o = dot(hid[:, 0:256], w2[0, b]) + dot(hid[:, 256:512], w2[1, b])
        return o * gate_s[:, 0:1]

    r_cps = {}

    def r_send(idx, src, dst, to):
        r_cps[idx] = send(src, dst, r_ss.at[idx], r_rs.at[idx], to)

    order = (2, 3, 1, 0)
    for i in order:
        outb[i, 2] = mm2(i, 2).astype(BF)
        r_send(4 * i, outb.at[i, 2, pl.ds(0, 64)], rs_h.at[i, 0], sdev(1))
        r_send(4 * i + 1, outb.at[i, 2, pl.ds(64, 64)], rs_h.at[i, 1], sdev(-1))
    for i in order:
        o1 = mm2(i, 1)
        o3 = mm2(i, 3)
        r_cps[4 * i].wait_recv()
        outb[i, 1, 0:64] = (o1[0:64] + rs_h[i, 0].astype(F32)).astype(BF)
        outb[i, 1, 64:128] = o1[64:128].astype(BF)
        r_send(4 * i + 2, outb.at[i, 1], rs_f.at[i, 0], sdev(1))
        r_cps[4 * i + 1].wait_recv()
        outb[i, 3, 0:64] = o3[0:64].astype(BF)
        outb[i, 3, 64:128] = (o3[64:128] + rs_h[i, 1].astype(F32)).astype(BF)
        r_send(4 * i + 3, outb.at[i, 3], rs_f.at[i, 1], sdev(-1))
        t_own[i] = mm2(i, 0)
    pump(3)

    def t_of(i):
        r_cps[4 * i + 2].wait_recv()
        r_cps[4 * i + 3].wait_recv()
        return t_own[i] + rs_f[i, 0].astype(F32) + rs_f[i, 1].astype(F32)

    t_sum[2] = t_of(2).astype(BF)
    r_send(16, t_sum.at[2, pl.ds(0, 64)], rp_h.at[0], pdev(1))
    r_send(17, t_sum.at[2, pl.ds(64, 64)], rp_h.at[1], pdev(-1))
    t3 = t_of(3)
    t1 = t_of(1)
    r_cps[17].wait_recv()
    t_sum[3, 0:64] = t3[0:64].astype(BF)
    t_sum[3, 64:128] = (t3[64:128] + rp_h[1].astype(F32)).astype(BF)
    r_send(18, t_sum.at[3], rp_f.at[1], pdev(-1))
    r_cps[16].wait_recv()
    t_sum[1, 0:64] = (t1[0:64] + rp_h[0].astype(F32)).astype(BF)
    t_sum[1, 64:128] = t1[64:128].astype(BF)
    r_send(19, t_sum.at[1], rp_f.at[0], pdev(1))
    attend_far(2)
    pump(4)
    t0 = t_of(0)
    r_cps[18].wait_recv()
    r_cps[19].wait_recv()
    e_buf[0, c] = (t0 + rp_f[0].astype(F32) + rp_f[1].astype(F32)).astype(BF)

    e_cps = {}
    ep_cps = {}

    def e_send(r_from, r_to, way, lo, hi):
        e_cps[r_to, way] = send(
            e_buf.at[r_from, c, pl.ds(lo, hi - lo)], e_buf.at[r_to, c, pl.ds(lo, hi - lo)],
            e_ss.at[r_to, way], e_rs.at[r_to, way], dev(dz=1 if way == 0 else -1),
        )

    def e_share(r):
        ep_cps[r] = send(e_buf.at[r, c], e_buf.at[r, c], ep_ss.at[r], ep_rs.at[r], partner)

    e_send(0, 1, 0, 0, 128)
    e_send(0, 7, 1, 0, 128)
    e_share(0)
    pump(5)
    attend_far(3)
    for d in (1, 2):
        e_cps[d, 0].wait_recv()
        e_send(d, d + 1, 0, 0, 128)
        e_cps[8 - d, 1].wait_recv()
        e_send(8 - d, 7 - d, 1, 0, 128)
        e_share(d)
        e_share(8 - d)
    pump(6)
    e_cps[3, 0].wait_recv()
    e_send(3, 4, 0, 0, 64)
    e_cps[5, 1].wait_recv()
    e_send(5, 4, 1, 64, 128)
    e_share(3)
    e_share(5)
    attend_far(4)

    seen = pos_row[0:1, :] <= lax.broadcasted_iota(jnp.int32, (256, 256), 0) + e * 256

    @pl.loop(0, 4)
    def _(h):
        hs = pl.ds(pl.multiple_of(h * 128, 128), 128)
        scores = dot_nt(qry[:, hs], kp[:, hs].astype(BF))
        w = jnp.exp((scores - mrow[h][:, 0:1]) * INV_ROOT)
        wp[h] = jnp.where(seen, w, 0.0).astype(BF)

    e_cps[4, 0].wait_recv()
    e_cps[4, 1].wait_recv()
    e_share(4)
    for r in range(8):
        ep_cps[r].wait_recv()
    for g in range(2):
        for h in range(2):
            total = None
            for plane in range(4 * g, 4 * g + 4):
                term = e_buf[lax.rem(z - plane + 8, 8), h].astype(F32)
                total = term if total is None else total + term
            u_buf[128 * g : 128 * g + 128, 256 * h : 256 * h + 256] = total.astype(BF)

    hit = pos_row[0:1, :] == lax.broadcasted_iota(jnp.int32, (256, 256), 0) + e * 256
    scatter = jnp.where(hit, 1.0, 0.0).astype(BF)
    mixed_o[...] = (tok[...].astype(F32) + dot(scatter, u_buf[...])).astype(BF)

    @pl.loop(0, 4)
    def _(h):
        hs = pl.ds(pl.multiple_of(h * 128, 128), 128)
        num = acc[:, hs] + dot(wp[h], u_buf[:, hs])
        den = jnp.sum(lrow[h], axis=1, keepdims=True)
        att_o[:, hs] = (num / den).astype(BF)

    for cp in sent:
        cp.wait_send()
    w2_far.wait_send()


def body(tokens, queries, attn_keys, router, w_in, w_out, pick_rows, counts):
    rt = jnp.pad(router.T[:, None, :], ((0, 0), (0, 15), (0, 0)))
    vm = pl.BlockSpec(memory_space=pltpu.VMEM)
    sm = pl.BlockSpec(memory_space=pltpu.SMEM)
    hbm = pl.BlockSpec(memory_space=pl.ANY)
    V = pltpu.VMEM
    S = pltpu.SemaphoreType.DMA
    out = jax.ShapeDtypeStruct((256, 512), BF)
    return pl.pallas_call(
        kernel,
        name="layer",
        out_shape=(out, out),
        in_specs=[vm, vm, vm, vm, hbm, hbm, sm, sm],
        out_specs=(vm, vm),
        scratch_shapes=[
            V((2, 2, 48, 128), BF),
            V((16, 48, 128), BF),
            V((16, BLOCK_ROWS, 256), BF),
            V((2, 16, 256, 256), BF),
            V((2, 16, 256, 256), BF),
            V((128, 640), F32),
            V((128, 640), F32),
            V((128, 16), F32),
            V((128, 512), BF),
            V((128, 128), F32),
            V((4, 4, 128, 256), BF),
            V((4, 128, 256), F32),
            V((4, 2, 64, 256), BF),
            V((4, 2, 128, 256), BF),
            V((4, 128, 256), BF),
            V((2, 64, 256), BF),
            V((2, 128, 256), BF),
            V((8, 2, 128, 256), BF),
            V((256, 512), BF),
            V((8, 2, 256, 512), BF),
            V((8, 2, 256, 512), BF),
            V((256, 512), F32),
            V((4, 256, 128), F32),
            V((4, 256, 128), F32),
            V((256, 512), F32),
            V((4, 256, 256), BF),
            V((256, 128), jnp.int32),
            V((8, 256), jnp.int32),
            S((2,)),
            S((16,)), S((16,)),
            S((2,)), S((2,)),
            S((20,)), S((20,)),
            S((1,)), S((1,)),
            S((20,)), S((20,)),
            S((8, 2)), S((8, 2)),
            S((8,)), S((8,)),
            S((2, 8, 2)), S((2, 8, 2)),
            S((2, 8)), S((2, 8)),
        ],
        compiler_params=pltpu.CompilerParams(
            collective_id=0, has_side_effects=True, vmem_limit_bytes=50 * 2**20
        ),
    )(
        tokens, queries, attn_keys, rt,
        w_in.reshape(16, 2, 256, 256), w_out, pick_rows, counts,
    )


def solution(mesh):
    placed = (
        P("expert", "mp"),
        P("expert", "mp"),
        P("expert", "mp"),
        P("mp", None),
        P(None, ("expert", "mp")),
        P(("expert", "mp"), None),
        P(None, "expert", None),
        P(None, "expert"),
    )
    return jax.shard_map(
        body,
        mesh=mesh,
        in_specs=placed,
        out_specs=(P("expert", "mp"), P("expert", "mp")),
        check_vma=False,
    )
```

```python
import jax
import jax.numpy as jnp
from jax import lax
from jax.experimental import pallas as pl
from jax.experimental.pallas import tpu as pltpu
from jax.sharding import PartitionSpec as P

MESH = pl.DeviceIdType.MESH
HEAD_DIM = 128
BF = jnp.bfloat16
F32 = jnp.float32
NT = (((1,), (1,)), ((), ()))
INV_ROOT = HEAD_DIM ** (-0.5)
BLOCK_ROWS = 144


def dot(a, b):
    return jnp.dot(a, b, preferred_element_type=F32)


def dot_nt(a, b):
    return lax.dot_general(a, b, NT, preferred_element_type=F32)


def kernel(
    tok_h, qry_h, key_h, rt, win, wout, picks, cnts, mixed_o, att_o,
    tok, qry, key,
    a_msg, a_buf, xg, w1, w2, part, part_in, lgacc, hid, gate_s,
    outb, rs_in, t_sum, rp_in, f_sum, f_out, e_in, u_buf,
    kb, vb, acc, mrow, lrow, kp, wp, pos_col, pos_row,
    loc_sem, a_ss, a_rs, w_ss, w_rs, g_ss, g_rs, x_ss, x_rs,
    r_ss, r_rs, e_ss, e_rs, ep_ss, ep_rs, kv_ss, kv_rs, kvp_ss, kvp_rs,
):
    e = lax.axis_index("expert")
    m = lax.axis_index("mp")
    z, c = e // 2, lax.rem(e, 2)
    y, x = m // 4, lax.rem(m, 4)
    oc = 1 - c
    group = z // 4

    def dev(dz=0, dc=0, dy=0, dx=0):
        zz = lax.rem(z + dz + 8, 8)
        cc = lax.rem(c + dc, 2)
        return (zz * 2 + cc, lax.rem(y + dy + 4, 4) * 4 + lax.rem(x + dx + 4, 4))

    def along(i, j):
        return c * i + oc * j, oc * i + c * j

    def blk(i, j):
        dy, dx = along(i, j)
        return lax.rem(y + dy + 4, 4) * 4 + lax.rem(x + dx + 4, 4)

    def pdev(d):
        dy, dx = along(d, 0)
        return dev(dy=dy, dx=dx)

    def sdev(d):
        dy, dx = along(0, d)
        return dev(dy=dy, dx=dx)

    partner = dev(dc=1)
    sent = []

    def send(src, dst, ss, rs, to):
        cp = pltpu.make_async_remote_copy(
            src_ref=src, dst_ref=dst, send_sem=ss, recv_sem=rs, device_id=to, device_id_type=MESH
        )
        cp.start()
        sent.append(cp)
        return cp

    tok_in = pltpu.make_async_copy(tok_h, tok, loc_sem.at[2])
    key_in = pltpu.make_async_copy(key_h, key, loc_sem.at[3])
    qry_in = pltpu.make_async_copy(qry_h, qry, loc_sem.at[4])
    tok_in.start()
    key_in.start()
    qry_in.start()
    w1_loc = pltpu.make_async_copy(win.at[:, c], w1.at[c], loc_sem.at[0])
    w1_loc.start()
    barrier = pltpu.get_barrier_semaphore()
    for dz in range(8):
        for dc in range(2):
            if dz or dc:
                pl.semaphore_signal(barrier, inc=1, device_id=dev(dz, dc), device_id_type=MESH)
    for d in (1, 2, 3):
        pl.semaphore_signal(barrier, inc=1, device_id=dev(dy=d), device_id_type=MESH)
        pl.semaphore_signal(barrier, inc=1, device_id=dev(dx=d), device_id_type=MESH)

    row32 = lax.broadcasted_iota(jnp.int32, (32, 256), 0)
    lane32 = lax.broadcasted_iota(jnp.int32, (32, 256), 1)
    chosen = jnp.full((32, 256), -1, jnp.int32)
    row16 = lax.broadcasted_iota(jnp.int32, (16, 128), 0)
    lane16 = lax.broadcasted_iota(jnp.int32, (16, 128), 1)
    meta = jnp.where(row16 == 0, cnts[0, 0], jnp.where(row16 == 1, cnts[0, 1], 0))
    base = 16 * lax.rem(e, 8)
    for g in range(2):
        for j in range(16):
            pick = picks[g, j]
            live = jnp.where(j < cnts[0, g], pick, -1)
            chosen = jnp.where(row32 == 16 * g + j, live, chosen)
            meta = jnp.where(
                (row16 == 2 + 2 * g + e // 8) & (lane16 == base + j), pick, meta
            )
    onehot = jnp.where(chosen == lane32, 1.0, 0.0).astype(BF)
    tok_in.wait()
    rows = dot(onehot, tok[...]).astype(BF)
    meta_b = meta.astype(F32).astype(BF)
    for g in range(2):
        for h in range(2):
            a_msg[g, h, 0:16, :] = rows[16 * g : 16 * g + 16, 256 * h : 256 * h + 128]
            a_msg[g, h, 16:32, :] = rows[16 * g : 16 * g + 16, 256 * h + 128 : 256 * h + 256]
            a_msg[g, h, 32:48, :] = meta_b
    a_buf[e] = a_msg[group, c]
    pl.semaphore_wait(barrier, 21)

    a_cps = []
    for dz in (4, 3, 5, 2, 6, 1, 7, 0):
        for dc in range(2):
            if dz or dc:
                to_plane = lax.rem(z + dz, 8)
                to_core = lax.rem(c + dc, 2)
                a_cps.append(
                    send(
                        a_msg.at[to_plane // 4, to_core], a_buf.at[e],
                        a_ss.at[dz * 2 + dc], a_rs.at[dz * 2 + dc], dev(dz, dc),
                    )
                )

    def kv_send(buf, which, r_from, r_to, way, src=None):
        src = buf.at[r_from, c] if src is None else src
        return send(
            src, buf.at[r_to, c], kv_ss.at[which, r_to, way], kv_rs.at[which, r_to, way],
            dev(dz=1 if way == 0 else -1),
        )

    def kv_share(buf, which, r, src=None):
        src = buf.at[r, c] if src is None else src
        return send(src, buf.at[r, c], kvp_ss.at[which, r], kvp_rs.at[which, r], partner)

    key_in.wait()
    qry_in.wait()
    pieces = {}
    shared = {}
    pieces["k", 1] = kv_send(kb, 0, 0, 1, 0, key)
    pieces["v", 7] = kv_send(vb, 1, 0, 7, 1, tok)
    shared["k", 0] = kv_share(kb, 0, 0, key)
    shared["v", 0] = kv_share(vb, 1, 0, tok)
    pieces["v", 1] = kv_send(vb, 1, 0, 1, 0, tok)
    pieces["k", 7] = kv_send(kb, 0, 0, 7, 1, key)
    right = [("k", 1), ("v", 1), ("k", 2), ("v", 2), ("k", 3), ("v", 3), ("k", 4)]
    left = [("v", 7), ("k", 7), ("v", 6), ("k", 6), ("v", 5), ("k", 5), ("v", 4)]

    def pump(n):
        for way, (what, r) in ((0, right[n]), (1, left[n])):
            pieces[what, r].wait_recv()
            which, buf = (0, kb) if what == "k" else (1, vb)
            r_to = r + 1 if way == 0 else r - 1
            if (what, r_to) in (right if way == 0 else left):
                pieces[what, r_to] = kv_send(buf, which, r, r_to, way)
            shared[what, r] = kv_share(buf, which, r)

    w1_far = send(win.at[:, oc], w1.at[c], w_ss.at[0], w_rs.at[0], partner)

    def w2_copies():
        for b in range(16):
            mine = pl.ds(pl.multiple_of(512 * b + 256 * c, 256), 256)
            pltpu.make_async_copy(wout.at[:, mine], w2.at[c, b], loc_sem.at[1]).start()
        for b in range(16):
            other = pl.ds(pl.multiple_of(512 * b + 256 * oc, 256), 256)
            pltpu.make_async_remote_copy(
                src_ref=wout.at[:, other], dst_ref=w2.at[c, b], send_sem=w_ss.at[1],
                recv_sem=w_rs.at[1], device_id=partner, device_id_type=MESH,
            ).start()

    w2_copies()
    w2_loc = pltpu.make_async_copy(w2.at[c], w2.at[c], loc_sem.at[1])
    w2_far = pltpu.make_async_remote_copy(
        src_ref=w2.at[c], dst_ref=w2.at[c], send_sem=w_ss.at[1], recv_sem=w_rs.at[1],
        device_id=partner, device_id_type=MESH,
    )

    def soft_step(h, scores, v_h):
        hs = pl.ds(pl.multiple_of(h * 128, 128), 128)
        old = mrow[h][:, 0:1]
        new = jnp.maximum(old, jnp.max(scores, axis=1, keepdims=True))
        alpha = jnp.exp((old - new) * INV_ROOT)
        w = jnp.exp((scores - new) * INV_ROOT)
        total = w[:, 0:128]
        for i in range(1, scores.shape[1] // 128):
            total = total + w[:, 128 * i : 128 * i + 128]
        lrow[h] = lrow[h] * alpha + total
        acc[:, hs] = acc[:, hs] * alpha + dot(w.astype(BF), v_h)
        mrow[h] = jnp.broadcast_to(new, (256, 128))

    def attend_own():
        allowed = lax.broadcasted_iota(jnp.int32, (256, 256), 1) <= lax.broadcasted_iota(
            jnp.int32, (256, 256), 0
        )

        @pl.loop(0, 4)
        def _(h):
            hs = pl.ds(pl.multiple_of(h * 128, 128), 128)
            scores = jnp.where(allowed, dot_nt(qry[:, hs], key[:, hs]), -1e30)
            new = jnp.max(scores, axis=1, keepdims=True)
            w = jnp.exp((scores - new) * INV_ROOT)
            lrow[h] = w[:, 0:128] + w[:, 128:256]
            acc[:, hs] = dot(w.astype(BF), tok[:, hs])
            mrow[h] = jnp.broadcast_to(new, (256, 128))

    def attend_partner():
        @pl.loop(0, 4)
        def _(h):
            hs = pl.ds(pl.multiple_of(h * 128, 128), 128)
            soft_step(h, dot_nt(qry[:, hs], kb[0, 0, :, hs]), vb[0, 0, :, hs])

    def attend_chip(r, first, last):
        @pl.loop(first, last)
        def _(h):
            hs = pl.ds(pl.multiple_of(h * 128, 128), 128)
            k_h = kb[r, :, :, hs].reshape(512, 128)
            v_h = vb[r, :, :, hs].reshape(512, 128)
            soft_step(h, dot_nt(qry[:, hs], k_h), v_h)

    def pick_keys(first, k_rows):
        n = k_rows.shape[0]
        at = lax.broadcasted_iota(jnp.int32, (256, n), 1) + first
        sel = jnp.where(pos_col[:, 0:1] == at, 1.0, 0.0).astype(BF)
        kp[...] += dot(sel, k_rows)

    def far_unit(d, side, part_no):
        r, ok = ((d, z >= d), (8 - d, z >= 8 - d))[side]
        if part_no == 0:
            for what in ("k", "v"):
                shared[what, r].wait_recv()

        @pl.when(ok)
        def _():
            if part_no < 2:
                attend_chip(r, 2 * part_no, 2 * part_no + 2)
            else:
                pick_keys((z - r) * 512, kb[r].reshape(512, 512))

    far = [(d, side, p) for d in (1, 2, 3) for side in (0, 1) for p in range(3)]
    far += [(4, 0, p) for p in range(3)]

    def fill(n):
        for _ in range(n):
            if far:
                far_unit(*far.pop(0))

    attend_own()
    for what in ("k", "v"):
        shared[what, 0].wait_recv()

    @pl.when(c == 1)
    def _():
        attend_partner()

    for cp in a_cps:
        cp.wait_recv()
    lane_f = lane16.astype(F32)
    run = jnp.zeros((16, 128), F32)
    slot_at = [jnp.full((16, 128), -1.0, F32), jnp.full((16, 128), -1.0, F32)]
    picked_lane = jnp.zeros((16, 128), F32)
    for s in range(16):
        t = a_buf[s, 32:48, :].astype(F32)
        j = lane_f - 16.0 * (s % 8)
        here = (lane16 // 16 == s % 8) & (j < t)
        slot_at[s // 8] = jnp.where(here, run + j, slot_at[s // 8])
        run = run + t
        picked_lane = picked_lane + t
    row_f = lax.broadcasted_iota(jnp.int32, (128, 256), 0).astype(F32)
    row_l = lax.broadcasted_iota(jnp.int32, (16, 256), 0)
    lane_l = lax.broadcasted_iota(jnp.int32, (16, 256), 1)
    compact = []
    for g in range(2):
        at = jnp.concatenate([slot_at[0][g : g + 1], slot_at[1][g : g + 1]], axis=1)
        cmat = jnp.where(row_f == at, 1.0, 0.0).astype(BF)
        compact.append(cmat)
    mine = jnp.where(group == 0, compact[0].astype(F32), compact[1].astype(F32)).astype(BF)
    for h in range(2):
        got = a_buf[:, 16 * h : 16 * h + 16, :].reshape(256, 128)
        xg[m, 0:128, 128 * h : 128 * h + 128] = dot(mine, got).astype(BF)
    half_lanes = pl.ds(pl.multiple_of(256 * c, 256), 256)
    rt_row = jnp.where(group == 0, rt[0:1, half_lanes].astype(F32), rt[1:2, half_lanes].astype(F32))
    xg[m, 128:144, :] = jnp.broadcast_to(rt_row, (16, 256)).astype(BF)

    g_cps = {}

    def g_send(idx, b, to):
        g_cps[idx] = send(xg.at[b], xg.at[b], g_ss.at[idx], g_rs.at[idx], to)

    def g_second(i):
        for d in (2, 1, 3):
            g_send(3 + 3 * i + d, blk(i, 0), sdev(d))

    def g_wait(i, j):
        if j:
            g_cps[7 + 3 * i - j].wait_recv()
        elif i:
            g_cps[4 - i].wait_recv()

    for d in (2, 1, 3):
        g_send(d, m, pdev(d))
    g_second(0)

    at_lane = []
    for g in range(2):
        pk = jnp.concatenate(
            [picked_lane[2 + 2 * g : 3 + 2 * g], picked_lane[3 + 2 * g : 4 + 2 * g]], axis=1
        )
        info = jnp.where(
            row_l == 0, jnp.broadcast_to(pk, (16, 256)), (lane_l // 16).astype(F32)
        ).astype(BF)
        col = dot_nt(compact[g], info)
        pos_col[128 * g : 128 * g + 128, :] = jnp.broadcast_to(
            (col[:, 0:1] + 256.0 * col[:, 1:2]).astype(jnp.int32), (128, 128)
        )
        lane = dot_nt(info, compact[g])
        at_lane.append((lane[0:1] + 256.0 * lane[1:2]).astype(jnp.int32))
    pos_row[...] = jnp.broadcast_to(jnp.concatenate(at_lane, axis=1), (8, 256))
    kp[...] = jnp.zeros((256, 512), F32)
    pick_keys(e * 256, key[...])

    @pl.when(c == 1)
    def _():
        pick_keys(z * 512, kb[0, 0])

    pump(0)
    part[...] = jnp.zeros((128, 640), F32)
    lgacc[...] = jnp.zeros((128, 16), F32)
    w1_loc.wait()
    w1_far.wait_recv()

    def mm1(i, j):
        b = blk(i, j)
        xb = xg[b, 0:128, :]
        part[:, 0:256] += dot(xb, w1[0, b])
        part[:, 256:512] += dot(xb, w1[1, b])
        lgacc[...] += dot_nt(xb, xg[b, 128:144, :])

    for i in (3, 1, 2):
        g_wait(i, 0)
        g_second(i)
    for i in (0, 3, 1, 2):
        mm1(i, 0)
    pump(1)
    for i in (0, 3, 1, 2):
        for j in (3, 1, 2):
            g_wait(i, j)
            mm1(i, j)

    part[:, 512:640] = jnp.broadcast_to(lgacc[:, 0:1], (128, 128))
    x_cp = send(part, part_in, x_ss.at[0], x_rs.at[0], partner)
    pump(2)
    fill(2)
    w2_loc.wait()
    w2_far.wait_recv()
    x_cp.wait_recv()
    hid[...] = jax.nn.gelu(part[:, 0:512] + part_in[:, 0:512]).astype(BF)
    gate_s[...] = jax.nn.sigmoid(part[:, 512:640] + part_in[:, 512:640])

    def mm2(i, j):
        b = blk(i, j)
        o = dot(hid[:, 0:256], w2[0, b]) + dot(hid[:, 256:512], w2[1, b])
        return o * gate_s[:, 0:1]

    r_cps = {}

    def r_send(idx, src, dst, to):
        r_cps[idx] = send(src, dst, r_ss.at[idx], r_rs.at[idx], to)

    for i in (2, 3, 1, 0):
        for j in (2, 3, 1):
            outb[i, j] = mm2(i, j).astype(BF)
            r_send(3 * i + j - 1, outb.at[i, j], rs_in.at[i, j - 1], sdev(j))
    pump(3)

    def t_of(i):
        total = mm2(i, 0)
        for j in (3, 1, 2):
            r_cps[3 * i + j - 1].wait_recv()
            total = total + rs_in[i, j - 1].astype(F32)
        return total

    for i in (2, 3, 1):
        t_sum[i] = t_of(i).astype(BF)
        r_send(11 + i, t_sum.at[i], rp_in.at[i - 1], pdev(i))
    full = t_of(0)
    fill(4)
    for i in (3, 1, 2):
        r_cps[11 + i].wait_recv()
        full = full + rp_in[i - 1].astype(F32)
    f_sum[...] = full
    f_out[...] = full.astype(BF)

    zz = lax.rem(z, 4)
    e_cps = []
    for d in (2, 1, 3):
        to_q = lax.rem(zz + d, 4)
        e_cps.append(
            send(
                f_out.at[pl.ds(pl.multiple_of(32 * to_q, 32), 32)], e_in.at[d - 1],
                e_ss.at[d - 1], e_rs.at[d - 1], ((4 * group + to_q) * 2 + c, m),
            )
        )
    pump(4)
    fill(2)
    total = f_sum[pl.ds(pl.multiple_of(32 * zz, 32), 32), :]
    for cp in e_cps:
        cp.wait_recv()
    for d in range(3):
        total = total + e_in[d].astype(F32)
    my_rows = pl.ds(pl.multiple_of(32 * z, 32), 32)
    u_buf[c, my_rows, :] = total.astype(BF)
    u_cps = []
    for d in (4, 3, 5, 2, 6, 1, 7):
        u_cps.append(
            send(
                u_buf.at[c, my_rows], u_buf.at[c, my_rows], e_ss.at[2 + d], e_rs.at[2 + d], dev(dz=d)
            )
        )
    pump(5)
    fill(4)
    pump(6)
    fill(len(far))

    seen = pos_row[0:1, :] <= lax.broadcasted_iota(jnp.int32, (256, 256), 0) + e * 256

    @pl.loop(0, 4)
    def _(h):
        hs = pl.ds(pl.multiple_of(h * 128, 128), 128)
        scores = dot_nt(qry[:, hs], kp[:, hs].astype(BF))
        w = jnp.exp((scores - mrow[h][:, 0:1]) * INV_ROOT)
        wp[h] = jnp.where(seen, w, 0.0).astype(BF)

    for cp in u_cps:
        cp.wait_recv()
    u_share = send(u_buf.at[c], u_buf.at[c], ep_ss.at[0], ep_rs.at[0], partner)
    u_share.wait_recv()

    hit = pos_row[0:1, :] == lax.broadcasted_iota(jnp.int32, (256, 256), 0) + e * 256
    scatter = jnp.where(hit, 1.0, 0.0).astype(BF)
    for h in range(2):
        cols = slice(256 * h, 256 * h + 256)
        mixed_o[:, cols] = (tok[:, cols].astype(F32) + dot(scatter, u_buf[h])).astype(BF)
    for h in range(4):
        cols = slice(128 * h, 128 * h + 128)
        u_h = u_buf[h // 2, :, 128 * (h % 2) : 128 * (h % 2) + 128]
        num = acc[:, cols] + dot(wp[h], u_h)
        den = jnp.sum(lrow[h], axis=1, keepdims=True)
        att_o[:, cols] = (num / den).astype(BF)

    for cp in sent:
        cp.wait_send()
    w2_far.wait_send()


def hand_over(mixed, attended, mixed_o, att_o, buf, sem):
    parts = [(a, b, i) for i in range(2) for a, b in ((mixed, mixed_o), (attended, att_o))]
    ins, outs = [], []
    for n, (a, b, i) in enumerate(parts):
        rows = pl.ds(128 * i, 128)
        ins.append(pltpu.make_async_copy(a.at[rows], buf.at[n], sem.at[n]))
        outs.append(pltpu.make_async_copy(buf.at[n], b.at[rows], sem.at[4 + n]))
    for cp in ins:
        cp.start()
    for i, cp in enumerate(ins):
        cp.wait()
        outs[i].start()
    for cp in outs:
        cp.wait()


def body(tokens, queries, attn_keys, router, w_in, w_out, pick_rows, counts):
    rt = router.T
    vm = pl.BlockSpec(memory_space=pltpu.VMEM)
    sm = pl.BlockSpec(memory_space=pltpu.SMEM)
    hbm = pl.BlockSpec(memory_space=pl.ANY)
    V = pltpu.VMEM
    S = pltpu.SemaphoreType.DMA
    out = jax.ShapeDtypeStruct((256, 512), BF)
    mixed, attended = pl.pallas_call(
        kernel,
        name="layer",
        out_shape=(out, out),
        in_specs=[hbm, hbm, hbm, vm, hbm, hbm, sm, sm],
        out_specs=(vm, vm),
        scratch_shapes=[
            V((256, 512), BF),
            V((256, 512), BF),
            V((256, 512), BF),
            V((2, 2, 48, 128), BF),
            V((16, 48, 128), BF),
            V((16, BLOCK_ROWS, 256), BF),
            V((2, 16, 256, 256), BF),
            V((2, 16, 256, 256), BF),
            V((128, 640), F32),
            V((128, 640), F32),
            V((128, 16), F32),
            V((128, 512), BF),
            V((128, 128), F32),
            V((4, 4, 128, 256), BF),
            V((4, 3, 128, 256), BF),
            V((4, 128, 256), BF),
            V((3, 128, 256), BF),
            V((128, 256), F32),
            V((128, 256), BF),
            V((3, 32, 256), BF),
            V((2, 256, 256), BF),
            V((8, 2, 256, 512), BF),
            V((8, 2, 256, 512), BF),
            V((256, 512), F32),
            V((4, 256, 128), F32),
            V((4, 256, 128), F32),
            V((256, 512), F32),
            V((4, 256, 256), BF),
            V((256, 128), jnp.int32),
            V((8, 256), jnp.int32),
            S((5,)),
            S((16,)), S((16,)),
            S((2,)), S((2,)),
            S((16,)), S((16,)),
            S((1,)), S((1,)),
            S((15,)), S((15,)),
            S((10,)), S((10,)),
            S((1,)), S((1,)),
            S((2, 8, 2)), S((2, 8, 2)),
            S((2, 8)), S((2, 8)),
        ],
        compiler_params=pltpu.CompilerParams(
            collective_id=0, has_side_effects=True, vmem_limit_bytes=58 * 2**20
        ),
    )(
        tokens, queries, attn_keys, rt,
        w_in.reshape(16, 2, 256, 256), w_out, pick_rows.reshape(2, 16), counts.reshape(1, 2),
    )
    return pl.pallas_call(
        hand_over,
        name="hand_over",
        out_shape=(out, out),
        in_specs=[hbm, hbm],
        out_specs=(hbm, hbm),
        scratch_shapes=[V((4, 128, 512), BF), S((8,))],
    )(mixed, attended)


def solution(mesh):
    placed = (
        P("expert", "mp"),
        P("expert", "mp"),
        P("expert", "mp"),
        P("mp", None),
        P(None, ("expert", "mp")),
        P(("expert", "mp"), None),
        P(None, "expert", None),
        P(None, "expert"),
    )
    return jax.shard_map(
        body,
        mesh=mesh,
        in_specs=placed,
        out_specs=(P("expert", "mp"), P("expert", "mp")),
        check_vma=False,
    )
```

```python
import jax
import jax.numpy as jnp
from jax import lax
from jax.experimental import pallas as pl
from jax.experimental.pallas import tpu as pltpu
from jax.sharding import PartitionSpec as P

MESH = pl.DeviceIdType.MESH
HEAD_DIM = 128
BF = jnp.bfloat16
F32 = jnp.float32
NT = (((1,), (1,)), ((), ()))
INV_ROOT = HEAD_DIM ** (-0.5) * 1.4426950408889634
BLOCK_ROWS = 144


def dot(a, b):
    return jnp.dot(a, b, preferred_element_type=F32)


def dot_nt(a, b):
    return lax.dot_general(a, b, NT, preferred_element_type=F32)


def kernel(
    tok_h, qry_h, key_h, rt, win, wout, picks, cnts, mixed_o, att_o,
    tok, qry, key,
    a_msg, a_buf, xg, w1, w2, part, part_in, lgacc, hid, gate_s,
    outb, rs_in, t_sum, rp_in, f_sum, f_out, e_in, u_buf,
    kb, vb, acc, mrow, lrow, kp, wp, pos_col, pos_row,
    loc_sem, a_ss, a_rs, w_ss, w_rs, g_ss, g_rs, x_ss, x_rs,
    r_ss, r_rs, e_ss, e_rs, ep_ss, ep_rs, kv_ss, kv_rs, kvp_ss, kvp_rs,
):
    e = lax.axis_index("expert")
    m = lax.axis_index("mp")
    z, c = e // 2, lax.rem(e, 2)
    y, x = m // 4, lax.rem(m, 4)
    oc = 1 - c
    group = z // 4

    def dev(dz=0, dc=0, dy=0, dx=0):
        zz = lax.rem(z + dz + 8, 8)
        cc = lax.rem(c + dc, 2)
        return (zz * 2 + cc, lax.rem(y + dy + 4, 4) * 4 + lax.rem(x + dx + 4, 4))

    def along(i, j):
        return c * i + oc * j, oc * i + c * j

    def blk(i, j):
        dy, dx = along(i, j)
        return lax.rem(y + dy + 4, 4) * 4 + lax.rem(x + dx + 4, 4)

    def pdev(d):
        dy, dx = along(d, 0)
        return dev(dy=dy, dx=dx)

    def sdev(d):
        dy, dx = along(0, d)
        return dev(dy=dy, dx=dx)

    partner = dev(dc=1)
    sent = []

    def send(src, dst, ss, rs, to):
        cp = pltpu.make_async_remote_copy(
            src_ref=src, dst_ref=dst, send_sem=ss, recv_sem=rs, device_id=to, device_id_type=MESH
        )
        cp.start()
        sent.append(cp)
        return cp

    tok_in = pltpu.make_async_copy(tok_h, tok, loc_sem.at[2])
    key_in = pltpu.make_async_copy(key_h, key, loc_sem.at[3])
    qry_in = pltpu.make_async_copy(qry_h, qry, loc_sem.at[4])
    tok_in.start()
    key_in.start()
    qry_in.start()
    w1_loc = pltpu.make_async_copy(win.at[:, c], w1.at[c], loc_sem.at[0])
    w1_loc.start()
    barrier = pltpu.get_barrier_semaphore()
    for dz in range(8):
        for dc in range(2):
            if dz or dc:
                pl.semaphore_signal(barrier, inc=1, device_id=dev(dz, dc), device_id_type=MESH)
    for d in (1, 2, 3):
        pl.semaphore_signal(barrier, inc=1, device_id=dev(dy=d), device_id_type=MESH)
        pl.semaphore_signal(barrier, inc=1, device_id=dev(dx=d), device_id_type=MESH)

    row32 = lax.broadcasted_iota(jnp.int32, (32, 256), 0)
    lane32 = lax.broadcasted_iota(jnp.int32, (32, 256), 1)
    chosen = jnp.full((32, 256), -1, jnp.int32)
    row16 = lax.broadcasted_iota(jnp.int32, (16, 128), 0)
    lane16 = lax.broadcasted_iota(jnp.int32, (16, 128), 1)
    meta = jnp.where(row16 == 0, cnts[0, 0], jnp.where(row16 == 1, cnts[0, 1], 0))
    base = 16 * lax.rem(e, 8)
    for g in range(2):
        for j in range(16):
            pick = picks[g, j]
            live = jnp.where(j < cnts[0, g], pick, -1)
            chosen = jnp.where(row32 == 16 * g + j, live, chosen)
            meta = jnp.where(
                (row16 == 2 + 2 * g + e // 8) & (lane16 == base + j), pick, meta
            )
    onehot = jnp.where(chosen == lane32, 1.0, 0.0).astype(BF)
    tok_in.wait()
    rows = dot(onehot, tok[...]).astype(BF)
    meta_b = meta.astype(F32).astype(BF)
    for g in range(2):
        for h in range(2):
            a_msg[g, h, 0:16, :] = rows[16 * g : 16 * g + 16, 256 * h : 256 * h + 128]
            a_msg[g, h, 16:32, :] = rows[16 * g : 16 * g + 16, 256 * h + 128 : 256 * h + 256]
            a_msg[g, h, 32:48, :] = meta_b
    a_buf[e] = a_msg[group, c]
    pl.semaphore_wait(barrier, 21)

    a_cps = []
    for dz in (4, 3, 5, 2, 6, 1, 7, 0):
        for dc in range(2):
            if dz or dc:
                to_plane = lax.rem(z + dz, 8)
                to_core = lax.rem(c + dc, 2)
                a_cps.append(
                    send(
                        a_msg.at[to_plane // 4, to_core], a_buf.at[e],
                        a_ss.at[dz * 2 + dc], a_rs.at[dz * 2 + dc], dev(dz, dc),
                    )
                )

    def kv_send(buf, which, r_from, r_to, way, src=None):
        src = buf.at[r_from, c] if src is None else src
        return send(
            src, buf.at[r_to, c], kv_ss.at[which, r_to, way], kv_rs.at[which, r_to, way],
            dev(dz=1 if way == 0 else -1),
        )

    def kv_share(buf, which, r, src=None):
        src = buf.at[r, c] if src is None else src
        return send(src, buf.at[r, c], kvp_ss.at[which, r], kvp_rs.at[which, r], partner)

    key_in.wait()
    qry_in.wait()
    pieces = {}
    shared = {}
    pieces["k", 1] = kv_send(kb, 0, 0, 1, 0, key)
    pieces["v", 7] = kv_send(vb, 1, 0, 7, 1, tok)
    shared["k", 0] = kv_share(kb, 0, 0, key)
    shared["v", 0] = kv_share(vb, 1, 0, tok)
    pieces["v", 1] = kv_send(vb, 1, 0, 1, 0, tok)
    pieces["k", 7] = kv_send(kb, 0, 0, 7, 1, key)
    right = [("k", 1), ("v", 1), ("k", 2), ("v", 2), ("k", 3), ("v", 3), ("k", 4)]
    left = [("v", 7), ("k", 7), ("v", 6), ("k", 6), ("v", 5), ("k", 5), ("v", 4)]

    def pump(n):
        for way, (what, r) in ((0, right[n]), (1, left[n])):
            pieces[what, r].wait_recv()
            which, buf = (0, kb) if what == "k" else (1, vb)
            r_to = r + 1 if way == 0 else r - 1
            if (what, r_to) in (right if way == 0 else left):
                pieces[what, r_to] = kv_send(buf, which, r, r_to, way)
            shared[what, r] = kv_share(buf, which, r)

    w1_far = send(win.at[:, oc], w1.at[c], w_ss.at[0], w_rs.at[0], partner)

    def w2_copies():
        for b in range(16):
            mine = pl.ds(pl.multiple_of(512 * b + 256 * c, 256), 256)
            pltpu.make_async_copy(wout.at[:, mine], w2.at[c, b], loc_sem.at[1]).start()
        for b in range(16):
            other = pl.ds(pl.multiple_of(512 * b + 256 * oc, 256), 256)
            pltpu.make_async_remote_copy(
                src_ref=wout.at[:, other], dst_ref=w2.at[c, b], send_sem=w_ss.at[1],
                recv_sem=w_rs.at[1], device_id=partner, device_id_type=MESH,
            ).start()

    w2_copies()
    w2_loc = pltpu.make_async_copy(w2.at[c], w2.at[c], loc_sem.at[1])
    w2_far = pltpu.make_async_remote_copy(
        src_ref=w2.at[c], dst_ref=w2.at[c], send_sem=w_ss.at[1], recv_sem=w_rs.at[1],
        device_id=partner, device_id_type=MESH,
    )

    def soft_step(h, scores, v_h):
        hs = pl.ds(pl.multiple_of(h * 128, 128), 128)
        old = mrow[h][:, 0:1]
        new = jnp.maximum(old, jnp.max(scores, axis=1, keepdims=True))
        alpha = jnp.exp2((old - new) * INV_ROOT)
        w = jnp.exp2((scores - new) * INV_ROOT)
        total = w[:, 0:128]
        for i in range(1, scores.shape[1] // 128):
            total = total + w[:, 128 * i : 128 * i + 128]
        lrow[h] = lrow[h] * alpha + total
        acc[:, hs] = acc[:, hs] * alpha + dot(w.astype(BF), v_h)
        mrow[h] = jnp.broadcast_to(new, (256, 128))

    def attend_own():
        allowed = lax.broadcasted_iota(jnp.int32, (256, 256), 1) <= lax.broadcasted_iota(
            jnp.int32, (256, 256), 0
        )

        @pl.loop(0, 4)
        def _(h):
            hs = pl.ds(pl.multiple_of(h * 128, 128), 128)
            scores = jnp.where(allowed, dot_nt(qry[:, hs], key[:, hs]), -1e30)
            new = jnp.max(scores, axis=1, keepdims=True)
            w = jnp.exp2((scores - new) * INV_ROOT)
            lrow[h] = w[:, 0:128] + w[:, 128:256]
            acc[:, hs] = dot(w.astype(BF), tok[:, hs])
            mrow[h] = jnp.broadcast_to(new, (256, 128))

    def attend_partner():
        @pl.loop(0, 4)
        def _(h):
            hs = pl.ds(pl.multiple_of(h * 128, 128), 128)
            soft_step(h, dot_nt(qry[:, hs], kb[0, 0, :, hs]), vb[0, 0, :, hs])

    def attend_chip(r, first, last):
        @pl.loop(first, last)
        def _(h):
            hs = pl.ds(pl.multiple_of(h * 128, 128), 128)
            k_h = kb[r, :, :, hs].reshape(512, 128)
            v_h = vb[r, :, :, hs].reshape(512, 128)
            soft_step(h, dot_nt(qry[:, hs], k_h), v_h)

    def pick_keys(first, k_rows):
        n = k_rows.shape[0]
        at = lax.broadcasted_iota(jnp.int32, (256, n), 1) + first
        sel = jnp.where(pos_col[:, 0:1] == at, 1.0, 0.0).astype(BF)
        kp[...] += dot(sel, k_rows)

    def far_unit(d, side, part_no):
        r, ok = ((d, z >= d), (8 - d, z >= 8 - d))[side]
        if part_no == 0:
            for what in ("k", "v"):
                shared[what, r].wait_recv()

        @pl.when(ok)
        def _():
            if part_no < 2:
                attend_chip(r, 2 * part_no, 2 * part_no + 2)
            else:
                pick_keys((z - r) * 512, kb[r].reshape(512, 512))

    far = [(d, side, p) for d in (1, 2, 3) for side in (0, 1) for p in range(3)]

    def fill(n):
        for _ in range(n):
            if far:
                far_unit(*far.pop(0))

    attend_own()
    for what in ("k", "v"):
        shared[what, 0].wait_recv()

    @pl.when(c == 1)
    def _():
        attend_partner()

    for cp in a_cps:
        cp.wait_recv()
    lane_f = lane16.astype(F32)
    run = jnp.zeros((16, 128), F32)
    slot_at = [jnp.full((16, 128), -1.0, F32), jnp.full((16, 128), -1.0, F32)]
    picked_lane = jnp.zeros((16, 128), F32)
    for s in range(16):
        t = a_buf[s, 32:48, :].astype(F32)
        j = lane_f - 16.0 * (s % 8)
        here = (lane16 // 16 == s % 8) & (j < t)
        slot_at[s // 8] = jnp.where(here, run + j, slot_at[s // 8])
        run = run + t
        picked_lane = picked_lane + t
    row_f = lax.broadcasted_iota(jnp.int32, (128, 256), 0).astype(F32)
    row_l = lax.broadcasted_iota(jnp.int32, (16, 256), 0)
    lane_l = lax.broadcasted_iota(jnp.int32, (16, 256), 1)
    compact = []
    for g in range(2):
        at = jnp.concatenate([slot_at[0][g : g + 1], slot_at[1][g : g + 1]], axis=1)
        cmat = jnp.where(row_f == at, 1.0, 0.0).astype(BF)
        compact.append(cmat)
    mine = jnp.where(group == 0, compact[0].astype(F32), compact[1].astype(F32)).astype(BF)
    for h in range(2):
        got = a_buf[:, 16 * h : 16 * h + 16, :].reshape(256, 128)
        xg[m, 0:128, 128 * h : 128 * h + 128] = dot(mine, got).astype(BF)
    half_lanes = pl.ds(pl.multiple_of(256 * c, 256), 256)
    rt_row = jnp.where(group == 0, rt[0:1, half_lanes].astype(F32), rt[1:2, half_lanes].astype(F32))
    xg[m, 128:144, :] = jnp.broadcast_to(rt_row, (16, 256)).astype(BF)

    g_cps = {}

    def g_send(idx, b, to):
        g_cps[idx] = send(xg.at[b], xg.at[b], g_ss.at[idx], g_rs.at[idx], to)

    def g_second(i):
        for d in (2, 1, 3):
            g_send(3 + 3 * i + d, blk(i, 0), sdev(d))

    def g_wait(i, j):
        if j:
            g_cps[7 + 3 * i - j].wait_recv()
        elif i:
            g_cps[4 - i].wait_recv()

    for d in (2, 1, 3):
        g_send(d, m, pdev(d))
    g_second(0)

    at_lane = []
    for g in range(2):
        pk = jnp.concatenate(
            [picked_lane[2 + 2 * g : 3 + 2 * g], picked_lane[3 + 2 * g : 4 + 2 * g]], axis=1
        )
        info = jnp.where(
            row_l == 0, jnp.broadcast_to(pk, (16, 256)), (lane_l // 16).astype(F32)
        ).astype(BF)
        col = dot_nt(compact[g], info)
        pos_col[128 * g : 128 * g + 128, :] = jnp.broadcast_to(
            (col[:, 0:1] + 256.0 * col[:, 1:2]).astype(jnp.int32), (128, 128)
        )
        lane = dot_nt(info, compact[g])
        at_lane.append((lane[0:1] + 256.0 * lane[1:2]).astype(jnp.int32))
    pos_row[...] = jnp.broadcast_to(jnp.concatenate(at_lane, axis=1), (8, 256))
    kp[...] = jnp.zeros((256, 512), F32)
    pick_keys(e * 256, key[...])

    @pl.when(c == 1)
    def _():
        pick_keys(z * 512, kb[0, 0])

    part[...] = jnp.zeros((128, 640), F32)
    lgacc[...] = jnp.zeros((128, 16), F32)
    w1_loc.wait()
    w1_far.wait_recv()

    def mm1(i, j):
        b = blk(i, j)
        xb = xg[b, 0:128, :]
        part[:, 0:256] += dot(xb, w1[0, b])
        part[:, 256:512] += dot(xb, w1[1, b])
        lgacc[...] += dot_nt(xb, xg[b, 128:144, :])

    for i in (3, 1, 2):
        g_wait(i, 0)
        g_second(i)
    for i in (0, 3, 1, 2):
        mm1(i, 0)
    pump(0)
    for i in (0, 3, 1, 2):
        for j in (3, 1, 2):
            g_wait(i, j)
            mm1(i, j)
        if i == 3:
            pump(1)

    part[:, 512:640] = jnp.broadcast_to(lgacc[:, 0:1], (128, 128))
    x_cp = send(part, part_in, x_ss.at[0], x_rs.at[0], partner)
    fill(2)
    pump(2)
    fill(1)
    w2_loc.wait()
    w2_far.wait_recv()
    x_cp.wait_recv()
    hid[...] = jax.nn.gelu(part[:, 0:512] + part_in[:, 0:512]).astype(BF)
    gate_s[...] = jax.nn.sigmoid(part[:, 512:640] + part_in[:, 512:640])

    def mm2(i, j):
        b = blk(i, j)
        o = dot(hid[:, 0:256], w2[0, b]) + dot(hid[:, 256:512], w2[1, b])
        return o * gate_s[:, 0:1]

    r_cps = {}

    def r_send(idx, src, dst, to):
        r_cps[idx] = send(src, dst, r_ss.at[idx], r_rs.at[idx], to)

    for i in (2, 3, 1, 0):
        for j in (2, 3, 1):
            outb[i, j] = mm2(i, j).astype(BF)
            r_send(3 * i + j - 1, outb.at[i, j], rs_in.at[i, j - 1], sdev(j))
    pump(3)
    fill(3)

    def t_of(i):
        total = mm2(i, 0)
        for j in (3, 1, 2):
            r_cps[3 * i + j - 1].wait_recv()
            total = total + rs_in[i, j - 1].astype(F32)
        return total

    for i in (2, 3, 1):
        t_sum[i] = t_of(i).astype(BF)
        r_send(11 + i, t_sum.at[i], rp_in.at[i - 1], pdev(i))
    full = t_of(0)
    fill(4)
    for i in (3, 1, 2):
        r_cps[11 + i].wait_recv()
        full = full + rp_in[i - 1].astype(F32)
    f_sum[...] = full
    f_out[...] = full.astype(BF)

    zz = lax.rem(z, 4)
    e_cps = []
    for d in (2, 1, 3):
        to_q = lax.rem(zz + d, 4)
        e_cps.append(
            send(
                f_out.at[pl.ds(pl.multiple_of(32 * to_q, 32), 32)], e_in.at[d - 1],
                e_ss.at[d - 1], e_rs.at[d - 1], ((4 * group + to_q) * 2 + c, m),
            )
        )
    pump(4)
    fill(2)
    total = f_sum[pl.ds(pl.multiple_of(32 * zz, 32), 32), :]
    for cp in e_cps:
        cp.wait_recv()
    for d in range(3):
        total = total + e_in[d].astype(F32)
    my_rows = pl.ds(pl.multiple_of(32 * z, 32), 32)
    u_buf[c, my_rows, :] = total.astype(BF)
    u_cps = []
    for d in (4, 3, 5, 2, 6, 1, 7):
        u_cps.append(
            send(
                u_buf.at[c, my_rows], u_buf.at[c, my_rows], e_ss.at[2 + d], e_rs.at[2 + d], dev(dz=d)
            )
        )
    pump(5)
    fill(3)
    pump(6)
    fill(len(far))

    def attend_opposite(core):
        @pl.when(z >= 4)
        def _():
            @pl.loop(0, 4)
            def _(h):
                hs = pl.ds(pl.multiple_of(h * 128, 128), 128)
                soft_step(h, dot_nt(qry[:, hs], kb[4, core, :, hs]), vb[4, core, :, hs])

    attend_opposite(c)
    shared["k", 4].wait_recv()
    shared["v", 4].wait_recv()
    attend_opposite(oc)

    @pl.when(z >= 4)
    def _():
        pick_keys((z - 4) * 512, kb[4].reshape(512, 512))


    seen = pos_row[0:1, :] <= lax.broadcasted_iota(jnp.int32, (256, 256), 0) + e * 256

    @pl.loop(0, 4)
    def _(h):
        hs = pl.ds(pl.multiple_of(h * 128, 128), 128)
        scores = dot_nt(qry[:, hs], kp[:, hs].astype(BF))
        w = jnp.exp2((scores - mrow[h][:, 0:1]) * INV_ROOT)
        wp[h] = jnp.where(seen, w, 0.0).astype(BF)

    for cp in u_cps:
        cp.wait_recv()
    u_share = send(u_buf.at[c], u_buf.at[c], ep_ss.at[0], ep_rs.at[0], partner)
    u_share.wait_recv()

    hit = pos_row[0:1, :] == lax.broadcasted_iota(jnp.int32, (256, 256), 0) + e * 256
    scatter = jnp.where(hit, 1.0, 0.0).astype(BF)
    for h in range(2):
        cols = slice(256 * h, 256 * h + 256)
        mixed_o[:, cols] = (tok[:, cols].astype(F32) + dot(scatter, u_buf[h])).astype(BF)
    for h in range(4):
        cols = slice(128 * h, 128 * h + 128)
        u_h = u_buf[h // 2, :, 128 * (h % 2) : 128 * (h % 2) + 128]
        num = acc[:, cols] + dot(wp[h], u_h)
        den = jnp.sum(lrow[h], axis=1, keepdims=True)
        att_o[:, cols] = (num / den).astype(BF)

    for cp in sent:
        cp.wait_send()
    w2_far.wait_send()


def hand_over(mixed, attended, mixed_o, att_o, buf, sem):
    parts = [(a, b, i) for i in range(2) for a, b in ((mixed, mixed_o), (attended, att_o))]
    ins, outs = [], []
    for n, (a, b, i) in enumerate(parts):
        rows = pl.ds(128 * i, 128)
        ins.append(pltpu.make_async_copy(a.at[rows], buf.at[n], sem.at[n]))
        outs.append(pltpu.make_async_copy(buf.at[n], b.at[rows], sem.at[4 + n]))
    for cp in ins:
        cp.start()
    for i, cp in enumerate(ins):
        cp.wait()
        outs[i].start()
    for cp in outs:
        cp.wait()


def body(tokens, queries, attn_keys, router, w_in, w_out, pick_rows, counts):
    rt = router.T
    vm = pl.BlockSpec(memory_space=pltpu.VMEM)
    sm = pl.BlockSpec(memory_space=pltpu.SMEM)
    hbm = pl.BlockSpec(memory_space=pl.ANY)
    V = pltpu.VMEM
    S = pltpu.SemaphoreType.DMA
    out = jax.ShapeDtypeStruct((256, 512), BF)
    mixed, attended = pl.pallas_call(
        kernel,
        name="layer",
        out_shape=(out, out),
        in_specs=[hbm, hbm, hbm, vm, hbm, hbm, sm, sm],
        out_specs=(vm, vm),
        scratch_shapes=[
            V((256, 512), BF),
            V((256, 512), BF),
            V((256, 512), BF),
            V((2, 2, 48, 128), BF),
            V((16, 48, 128), BF),
            V((16, BLOCK_ROWS, 256), BF),
            V((2, 16, 256, 256), BF),
            V((2, 16, 256, 256), BF),
            V((128, 640), F32),
            V((128, 640), F32),
            V((128, 16), F32),
            V((128, 512), BF),
            V((128, 128), F32),
            V((4, 4, 128, 256), BF),
            V((4, 3, 128, 256), BF),
            V((4, 128, 256), BF),
            V((3, 128, 256), BF),
            V((128, 256), F32),
            V((128, 256), BF),
            V((3, 32, 256), BF),
            V((2, 256, 256), BF),
            V((8, 2, 256, 512), BF),
            V((8, 2, 256, 512), BF),
            V((256, 512), F32),
            V((4, 256, 128), F32),
            V((4, 256, 128), F32),
            V((256, 512), F32),
            V((4, 256, 256), BF),
            V((256, 128), jnp.int32),
            V((8, 256), jnp.int32),
            S((5,)),
            S((16,)), S((16,)),
            S((2,)), S((2,)),
            S((16,)), S((16,)),
            S((1,)), S((1,)),
            S((15,)), S((15,)),
            S((10,)), S((10,)),
            S((1,)), S((1,)),
            S((2, 8, 2)), S((2, 8, 2)),
            S((2, 8)), S((2, 8)),
        ],
        compiler_params=pltpu.CompilerParams(
            collective_id=0, has_side_effects=True, vmem_limit_bytes=58 * 2**20
        ),
    )(
        tokens, queries, attn_keys, rt,
        w_in.reshape(16, 2, 256, 256), w_out, pick_rows.reshape(2, 16), counts.reshape(1, 2),
    )
    return pl.pallas_call(
        hand_over,
        name="hand_over",
        out_shape=(out, out),
        in_specs=[hbm, hbm],
        out_specs=(hbm, hbm),
        scratch_shapes=[V((4, 128, 512), BF), S((8,))],
    )(mixed, attended)


def solution(mesh):
    placed = (
        P("expert", "mp"),
        P("expert", "mp"),
        P("expert", "mp"),
        P("mp", None),
        P(None, ("expert", "mp")),
        P(("expert", "mp"), None),
        P(None, "expert", None),
        P(None, "expert"),
    )
    return jax.shard_map(
        body,
        mesh=mesh,
        in_specs=placed,
        out_specs=(P("expert", "mp"), P("expert", "mp")),
        check_vma=False,
    )
```

```python
import jax
import jax.numpy as jnp
from jax import lax
from jax.experimental import pallas as pl
from jax.experimental.pallas import tpu as pltpu
from jax.sharding import PartitionSpec as P

MESH = pl.DeviceIdType.MESH
HEAD_DIM = 128
BF = jnp.bfloat16
F32 = jnp.float32
NT = (((1,), (1,)), ((), ()))
INV_ROOT = HEAD_DIM ** (-0.5) * 1.4426950408889634
BLOCK_ROWS = 144


def dot(a, b):
    return jnp.dot(a, b, preferred_element_type=F32)


def dot_nt(a, b):
    return lax.dot_general(a, b, NT, preferred_element_type=F32)


def kernel(
    tok_h, qry_h, key_h, rt, win, wout, picks, cnts, mixed_o, att_o,
    tok, qry, key,
    a_msg, a_buf, xg, w1, w2, part, part_in, lgacc, hid, gate_s,
    outb, rs_in, t_sum, rp_in, f_sum, f_out, e_in, u_buf,
    kb, vb, acc, mrow, lrow, kp, wp, pos_col, pos_row,
    loc_sem, a_ss, a_rs, w_ss, w_rs, g_ss, g_rs, x_ss, x_rs,
    r_ss, r_rs, e_ss, e_rs, ep_ss, ep_rs, kv_ss, kv_rs, kvp_ss, kvp_rs,
):
    e = lax.axis_index("expert")
    m = lax.axis_index("mp")
    z, c = e // 2, lax.rem(e, 2)
    y, x = m // 4, lax.rem(m, 4)
    oc = 1 - c
    group = z // 4

    def dev(dz=0, dc=0, dy=0, dx=0):
        zz = lax.rem(z + dz + 8, 8)
        cc = lax.rem(c + dc, 2)
        return (zz * 2 + cc, lax.rem(y + dy + 4, 4) * 4 + lax.rem(x + dx + 4, 4))

    def along(i, j):
        return c * i + oc * j, oc * i + c * j

    def blk(i, j):
        dy, dx = along(i, j)
        return lax.rem(y + dy + 4, 4) * 4 + lax.rem(x + dx + 4, 4)

    def pdev(d):
        dy, dx = along(d, 0)
        return dev(dy=dy, dx=dx)

    def sdev(d):
        dy, dx = along(0, d)
        return dev(dy=dy, dx=dx)

    partner = dev(dc=1)
    sent = []

    def send(src, dst, ss, rs, to):
        cp = pltpu.make_async_remote_copy(
            src_ref=src, dst_ref=dst, send_sem=ss, recv_sem=rs, device_id=to, device_id_type=MESH
        )
        cp.start()
        sent.append(cp)
        return cp

    tok_in = pltpu.make_async_copy(tok_h, tok, loc_sem.at[2])
    key_in = pltpu.make_async_copy(key_h, key, loc_sem.at[3])
    qry_in = pltpu.make_async_copy(qry_h, qry, loc_sem.at[4])
    tok_in.start()
    key_in.start()
    qry_in.start()
    w1_loc = pltpu.make_async_copy(win.at[:, c], w1.at[c], loc_sem.at[0])
    w1_loc.start()
    barrier = pltpu.get_barrier_semaphore()
    for dz in range(8):
        for dc in range(2):
            if dz or dc:
                pl.semaphore_signal(barrier, inc=1, device_id=dev(dz, dc), device_id_type=MESH)
    for d in (1, 2, 3):
        pl.semaphore_signal(barrier, inc=1, device_id=dev(dy=d), device_id_type=MESH)
        pl.semaphore_signal(barrier, inc=1, device_id=dev(dx=d), device_id_type=MESH)

    row32 = lax.broadcasted_iota(jnp.int32, (32, 256), 0)
    lane32 = lax.broadcasted_iota(jnp.int32, (32, 256), 1)
    chosen = jnp.full((32, 256), -1, jnp.int32)
    row16 = lax.broadcasted_iota(jnp.int32, (16, 128), 0)
    lane16 = lax.broadcasted_iota(jnp.int32, (16, 128), 1)
    meta = jnp.where(row16 == 0, cnts[0, 0], jnp.where(row16 == 1, cnts[0, 1], 0))
    base = 16 * lax.rem(e, 8)
    for g in range(2):
        for j in range(16):
            pick = picks[g, j]
            live = jnp.where(j < cnts[0, g], pick, -1)
            chosen = jnp.where(row32 == 16 * g + j, live, chosen)
            meta = jnp.where(
                (row16 == 2 + 2 * g + e // 8) & (lane16 == base + j), pick, meta
            )
    onehot = jnp.where(chosen == lane32, 1.0, 0.0).astype(BF)
    tok_in.wait()
    rows = dot(onehot, tok[...]).astype(BF)
    meta_b = meta.astype(F32).astype(BF)
    for g in range(2):
        for h in range(2):
            a_msg[g, h, 0:16, :] = rows[16 * g : 16 * g + 16, 256 * h : 256 * h + 128]
            a_msg[g, h, 16:32, :] = rows[16 * g : 16 * g + 16, 256 * h + 128 : 256 * h + 256]
            a_msg[g, h, 32:48, :] = meta_b
    a_buf[e] = a_msg[group, c]
    pl.semaphore_wait(barrier, 21)

    a_cps = []
    for dz in (4, 3, 5, 2, 6, 1, 7, 0):
        for dc in range(2):
            if dz or dc:
                to_plane = lax.rem(z + dz, 8)
                to_core = lax.rem(c + dc, 2)
                a_cps.append(
                    send(
                        a_msg.at[to_plane // 4, to_core], a_buf.at[e],
                        a_ss.at[dz * 2 + dc], a_rs.at[dz * 2 + dc], dev(dz, dc),
                    )
                )

    def kv_send(buf, which, r_from, r_to, way, src=None):
        src = buf.at[r_from, c] if src is None else src
        return send(
            src, buf.at[r_to, c], kv_ss.at[which, r_to, way], kv_rs.at[which, r_to, way],
            dev(dz=1 if way == 0 else -1),
        )

    def kv_share(buf, which, r, src=None):
        src = buf.at[r, c] if src is None else src
        return send(src, buf.at[r, c], kvp_ss.at[which, r], kvp_rs.at[which, r], partner)

    key_in.wait()
    qry_in.wait()
    pieces = {}
    shared = {}
    pieces["k", 1] = kv_send(kb, 0, 0, 1, 0, key)
    pieces["v", 7] = kv_send(vb, 1, 0, 7, 1, tok)
    shared["k", 0] = kv_share(kb, 0, 0, key)
    shared["v", 0] = kv_share(vb, 1, 0, tok)
    pieces["v", 1] = kv_send(vb, 1, 0, 1, 0, tok)
    pieces["k", 7] = kv_send(kb, 0, 0, 7, 1, key)
    right = [("k", 1), ("v", 1), ("k", 2), ("v", 2), ("k", 3), ("v", 3), ("k", 4)]
    left = [("v", 7), ("k", 7), ("v", 6), ("k", 6), ("v", 5), ("k", 5), ("v", 4)]

    def pump(n):
        for way, (what, r) in ((0, right[n]), (1, left[n])):
            pieces[what, r].wait_recv()
            which, buf = (0, kb) if what == "k" else (1, vb)
            r_to = r + 1 if way == 0 else r - 1
            if (what, r_to) in (right if way == 0 else left):
                pieces[what, r_to] = kv_send(buf, which, r, r_to, way)
            shared[what, r] = kv_share(buf, which, r)

    w1_far = send(win.at[:, oc], w1.at[c], w_ss.at[0], w_rs.at[0], partner)

    def w2_copies():
        for b in range(16):
            mine = pl.ds(pl.multiple_of(512 * b + 256 * c, 256), 256)
            pltpu.make_async_copy(wout.at[:, mine], w2.at[c, b], loc_sem.at[1]).start()
        for b in range(16):
            other = pl.ds(pl.multiple_of(512 * b + 256 * oc, 256), 256)
            pltpu.make_async_remote_copy(
                src_ref=wout.at[:, other], dst_ref=w2.at[c, b], send_sem=w_ss.at[1],
                recv_sem=w_rs.at[1], device_id=partner, device_id_type=MESH,
            ).start()

    w2_copies()
    w2_loc = pltpu.make_async_copy(w2.at[c], w2.at[c], loc_sem.at[1])
    w2_far = pltpu.make_async_remote_copy(
        src_ref=w2.at[c], dst_ref=w2.at[c], send_sem=w_ss.at[1], recv_sem=w_rs.at[1],
        device_id=partner, device_id_type=MESH,
    )

    def soft_step(h, scores, v_h):
        hs = pl.ds(pl.multiple_of(h * 128, 128), 128)
        old = mrow[h][:, 0:1]
        new = jnp.maximum(old, jnp.max(scores, axis=1, keepdims=True))
        alpha = jnp.exp2((old - new) * INV_ROOT)
        w = jnp.exp2((scores - new) * INV_ROOT)
        total = w[:, 0:128]
        for i in range(1, scores.shape[1] // 128):
            total = total + w[:, 128 * i : 128 * i + 128]
        lrow[h] = lrow[h] * alpha + total
        acc[:, hs] = acc[:, hs] * alpha + dot(w.astype(BF), v_h)
        mrow[h] = jnp.broadcast_to(new, (256, 128))

    def attend_own():
        allowed = lax.broadcasted_iota(jnp.int32, (256, 256), 1) <= lax.broadcasted_iota(
            jnp.int32, (256, 256), 0
        )

        @pl.loop(0, 4)
        def _(h):
            hs = pl.ds(pl.multiple_of(h * 128, 128), 128)
            scores = jnp.where(allowed, dot_nt(qry[:, hs], key[:, hs]), -1e30)
            new = jnp.max(scores, axis=1, keepdims=True)
            w = jnp.exp2((scores - new) * INV_ROOT)
            lrow[h] = w[:, 0:128] + w[:, 128:256]
            acc[:, hs] = dot(w.astype(BF), tok[:, hs])
            mrow[h] = jnp.broadcast_to(new, (256, 128))

    def attend_partner():
        @pl.loop(0, 4)
        def _(h):
            hs = pl.ds(pl.multiple_of(h * 128, 128), 128)
            soft_step(h, dot_nt(qry[:, hs], kb[0, 0, :, hs]), vb[0, 0, :, hs])

    def attend_chip(r, first, last):
        @pl.loop(first, last)
        def _(h):
            hs = pl.ds(pl.multiple_of(h * 128, 128), 128)
            k_h = kb[r, :, :, hs].reshape(512, 128)
            v_h = vb[r, :, :, hs].reshape(512, 128)
            soft_step(h, dot_nt(qry[:, hs], k_h), v_h)

    def pick_keys(first, k_rows):
        n = k_rows.shape[0]
        at = lax.broadcasted_iota(jnp.int32, (256, n), 1) + first
        sel = jnp.where(pos_col[:, 0:1] == at, 1.0, 0.0).astype(BF)
        kp[...] += dot(sel, k_rows)

    def far_unit(d, side, part_no):
        r, ok = ((d, z >= d), (8 - d, z >= 8 - d))[side]
        if part_no == 0:
            for what in ("k", "v"):
                shared[what, r].wait_recv()

        @pl.when(ok)
        def _():
            if part_no < 2:
                attend_chip(r, 2 * part_no, 2 * part_no + 2)
            else:
                pick_keys((z - r) * 512, kb[r].reshape(512, 512))

    far = [(d, side, p) for d in (1, 2, 3) for side in (0, 1) for p in range(3)]

    def fill(n):
        for _ in range(n):
            if far:
                far_unit(*far.pop(0))

    attend_own()
    for what in ("k", "v"):
        shared[what, 0].wait_recv()

    @pl.when(c == 1)
    def _():
        attend_partner()

    for cp in a_cps:
        cp.wait_recv()
    lane_f = lane16.astype(F32)
    run = jnp.zeros((16, 128), F32)
    slot_at = [jnp.full((16, 128), -1.0, F32), jnp.full((16, 128), -1.0, F32)]
    picked_lane = jnp.zeros((16, 128), F32)
    for s in range(16):
        t = a_buf[s, 32:48, :].astype(F32)
        j = lane_f - 16.0 * (s % 8)
        here = (lane16 // 16 == s % 8) & (j < t)
        slot_at[s // 8] = jnp.where(here, run + j, slot_at[s // 8])
        run = run + t
        picked_lane = picked_lane + t
    row_f = lax.broadcasted_iota(jnp.int32, (128, 256), 0).astype(F32)
    row_l = lax.broadcasted_iota(jnp.int32, (16, 256), 0)
    lane_l = lax.broadcasted_iota(jnp.int32, (16, 256), 1)
    compact = []
    for g in range(2):
        at = jnp.concatenate([slot_at[0][g : g + 1], slot_at[1][g : g + 1]], axis=1)
        cmat = jnp.where(row_f == at, 1.0, 0.0).astype(BF)
        compact.append(cmat)
    mine = jnp.where(group == 0, compact[0].astype(F32), compact[1].astype(F32)).astype(BF)
    for h in range(2):
        got = a_buf[:, 16 * h : 16 * h + 16, :].reshape(256, 128)
        xg[m, 0:128, 128 * h : 128 * h + 128] = dot(mine, got).astype(BF)
    half_lanes = pl.ds(pl.multiple_of(256 * c, 256), 256)
    rt_row = jnp.where(group == 0, rt[0:1, half_lanes].astype(F32), rt[1:2, half_lanes].astype(F32))
    xg[m, 128:144, :] = jnp.broadcast_to(rt_row, (16, 256)).astype(BF)

    g_cps = {}

    def g_send(idx, b, to):
        g_cps[idx] = send(xg.at[b], xg.at[b], g_ss.at[idx], g_rs.at[idx], to)

    def g_second(i):
        for d in (2, 1, 3):
            g_send(3 + 3 * i + d, blk(i, 0), sdev(d))

    def g_wait(i, j):
        if j:
            g_cps[7 + 3 * i - j].wait_recv()
        elif i:
            g_cps[4 - i].wait_recv()

    for d in (2, 1, 3):
        g_send(d, m, pdev(d))
    g_second(0)

    at_lane = []
    for g in range(2):
        pk = jnp.concatenate(
            [picked_lane[2 + 2 * g : 3 + 2 * g], picked_lane[3 + 2 * g : 4 + 2 * g]], axis=1
        )
        info = jnp.where(
            row_l == 0, jnp.broadcast_to(pk, (16, 256)), (lane_l // 16).astype(F32)
        ).astype(BF)
        col = dot_nt(compact[g], info)
        pos_col[128 * g : 128 * g + 128, :] = jnp.broadcast_to(
            (col[:, 0:1] + 256.0 * col[:, 1:2]).astype(jnp.int32), (128, 128)
        )
        lane = dot_nt(info, compact[g])
        at_lane.append((lane[0:1] + 256.0 * lane[1:2]).astype(jnp.int32))
    pos_row[...] = jnp.broadcast_to(jnp.concatenate(at_lane, axis=1), (8, 256))
    kp[...] = jnp.zeros((256, 512), F32)
    pick_keys(e * 256, key[...])

    @pl.when(c == 1)
    def _():
        pick_keys(z * 512, kb[0, 0])

    part[...] = jnp.zeros((128, 640), F32)
    lgacc[...] = jnp.zeros((128, 16), F32)
    w1_loc.wait()
    w1_far.wait_recv()

    def mm1(i, j):
        b = blk(i, j)
        xb = xg[b, 0:128, :]
        part[:, 0:256] += dot(xb, w1[0, b])
        part[:, 256:512] += dot(xb, w1[1, b])
        lgacc[...] += dot_nt(xb, xg[b, 128:144, :])

    for i in (3, 1, 2):
        g_wait(i, 0)
        g_second(i)
    for i in (0, 3, 1, 2):
        mm1(i, 0)
    pump(0)
    for i in (0, 3, 1, 2):
        for j in (3, 1, 2):
            g_wait(i, j)
            mm1(i, j)
        if i == 3:
            pump(1)

    part[:, 512:640] = jnp.broadcast_to(lgacc[:, 0:1], (128, 128))
    x_cp = send(part, part_in, x_ss.at[0], x_rs.at[0], partner)
    fill(2)
    pump(2)
    fill(1)
    w2_loc.wait()
    w2_far.wait_recv()
    x_cp.wait_recv()
    hid[...] = jax.nn.gelu(part[:, 0:512] + part_in[:, 0:512]).astype(BF)
    gate_s[...] = jax.nn.sigmoid(part[:, 512:640] + part_in[:, 512:640])

    def mm2(i, j):
        b = blk(i, j)
        o = dot(hid[:, 0:256], w2[0, b]) + dot(hid[:, 256:512], w2[1, b])
        return o * gate_s[:, 0:1]

    r_cps = {}

    def r_send(idx, src, dst, to):
        r_cps[idx] = send(src, dst, r_ss.at[idx], r_rs.at[idx], to)

    for i in (2, 3, 1, 0):
        for j in (2, 3, 1):
            outb[i, j] = mm2(i, j).astype(BF)
            r_send(3 * i + j - 1, outb.at[i, j], rs_in.at[i, j - 1], sdev(j))
    pump(3)
    fill(3)

    def t_of(i):
        total = mm2(i, 0)
        for j in (3, 1, 2):
            r_cps[3 * i + j - 1].wait_recv()
            total = total + rs_in[i, j - 1].astype(F32)
        return total

    for i in (2, 3, 1):
        t_sum[i] = t_of(i).astype(BF)
        r_send(11 + i, t_sum.at[i], rp_in.at[i - 1], pdev(i))
    full = t_of(0)
    fill(4)
    for i in (3, 1, 2):
        r_cps[11 + i].wait_recv()
        full = full + rp_in[i - 1].astype(F32)
    f_sum[...] = full
    f_out[...] = full.astype(BF)

    zz = lax.rem(z, 4)
    e_cps = []
    for d in (2, 1, 3):
        to_q = lax.rem(zz + d, 4)
        e_cps.append(
            send(
                f_out.at[pl.ds(pl.multiple_of(32 * to_q, 32), 32)], e_in.at[d - 1],
                e_ss.at[d - 1], e_rs.at[d - 1], ((4 * group + to_q) * 2 + c, m),
            )
        )
    pump(4)
    fill(2)
    total = f_sum[pl.ds(pl.multiple_of(32 * zz, 32), 32), :]
    for cp in e_cps:
        cp.wait_recv()
    for d in range(3):
        total = total + e_in[d].astype(F32)
    my_rows = pl.ds(pl.multiple_of(32 * z, 32), 32)
    u_buf[c, my_rows, :] = total.astype(BF)
    u_cps = []
    for d in (4, 3, 5, 2, 6, 1, 7):
        u_cps.append(
            send(
                u_buf.at[c, my_rows], u_buf.at[c, my_rows], e_ss.at[2 + d], e_rs.at[2 + d], dev(dz=d)
            )
        )
    pump(5)
    fill(5)
    pump(6)
    fill(len(far))

    def attend_opposite(core):
        @pl.when(z >= 4)
        def _():
            @pl.loop(0, 4)
            def _(h):
                hs = pl.ds(pl.multiple_of(h * 128, 128), 128)
                soft_step(h, dot_nt(qry[:, hs], kb[4, core, :, hs]), vb[4, core, :, hs])

    attend_opposite(c)
    shared["k", 4].wait_recv()
    shared["v", 4].wait_recv()
    attend_opposite(oc)

    @pl.when(z >= 4)
    def _():
        pick_keys((z - 4) * 512, kb[4].reshape(512, 512))


    seen = pos_row[0:1, :] <= lax.broadcasted_iota(jnp.int32, (256, 256), 0) + e * 256

    @pl.loop(0, 4)
    def _(h):
        hs = pl.ds(pl.multiple_of(h * 128, 128), 128)
        scores = dot_nt(qry[:, hs], kp[:, hs].astype(BF))
        w = jnp.exp2((scores - mrow[h][:, 0:1]) * INV_ROOT)
        wp[h] = jnp.where(seen, w, 0.0).astype(BF)

    for cp in u_cps:
        cp.wait_recv()
    u_share = send(u_buf.at[c], u_buf.at[c], ep_ss.at[0], ep_rs.at[0], partner)
    u_share.wait_recv()

    hit = pos_row[0:1, :] == lax.broadcasted_iota(jnp.int32, (256, 256), 0) + e * 256
    scatter = jnp.where(hit, 1.0, 0.0).astype(BF)
    for h in range(2):
        cols = slice(256 * h, 256 * h + 256)
        mixed_o[:, cols] = (tok[:, cols].astype(F32) + dot(scatter, u_buf[h])).astype(BF)
    for h in range(4):
        cols = slice(128 * h, 128 * h + 128)
        u_h = u_buf[h // 2, :, 128 * (h % 2) : 128 * (h % 2) + 128]
        num = acc[:, cols] + dot(wp[h], u_h)
        den = jnp.sum(lrow[h], axis=1, keepdims=True)
        att_o[:, cols] = (num / den).astype(BF)

    for cp in sent:
        cp.wait_send()
    w2_far.wait_send()


def hand_over(mixed, attended, mixed_o, att_o, buf, sem):
    parts = [(a, b, i) for i in range(2) for a, b in ((mixed, mixed_o), (attended, att_o))]
    ins, outs = [], []
    for n, (a, b, i) in enumerate(parts):
        rows = pl.ds(128 * i, 128)
        ins.append(pltpu.make_async_copy(a.at[rows], buf.at[n], sem.at[n]))
        outs.append(pltpu.make_async_copy(buf.at[n], b.at[rows], sem.at[4 + n]))
    for cp in ins:
        cp.start()
    for i, cp in enumerate(ins):
        cp.wait()
        outs[i].start()
    for cp in outs:
        cp.wait()


def body(tokens, queries, attn_keys, router, w_in, w_out, pick_rows, counts):
    rt = router.T
    vm = pl.BlockSpec(memory_space=pltpu.VMEM)
    sm = pl.BlockSpec(memory_space=pltpu.SMEM)
    hbm = pl.BlockSpec(memory_space=pl.ANY)
    V = pltpu.VMEM
    S = pltpu.SemaphoreType.DMA
    out = jax.ShapeDtypeStruct((256, 512), BF)
    mixed, attended = pl.pallas_call(
        kernel,
        name="layer",
        out_shape=(out, out),
        in_specs=[hbm, hbm, hbm, vm, hbm, hbm, sm, sm],
        out_specs=(vm, vm),
        scratch_shapes=[
            V((256, 512), BF),
            V((256, 512), BF),
            V((256, 512), BF),
            V((2, 2, 48, 128), BF),
            V((16, 48, 128), BF),
            V((16, BLOCK_ROWS, 256), BF),
            V((2, 16, 256, 256), BF),
            V((2, 16, 256, 256), BF),
            V((128, 640), F32),
            V((128, 640), F32),
            V((128, 16), F32),
            V((128, 512), BF),
            V((128, 128), F32),
            V((4, 4, 128, 256), BF),
            V((4, 3, 128, 256), BF),
            V((4, 128, 256), BF),
            V((3, 128, 256), BF),
            V((128, 256), F32),
            V((128, 256), BF),
            V((3, 32, 256), BF),
            V((2, 256, 256), BF),
            V((8, 2, 256, 512), BF),
            V((8, 2, 256, 512), BF),
            V((256, 512), F32),
            V((4, 256, 128), F32),
            V((4, 256, 128), F32),
            V((256, 512), F32),
            V((4, 256, 256), BF),
            V((256, 128), jnp.int32),
            V((8, 256), jnp.int32),
            S((5,)),
            S((16,)), S((16,)),
            S((2,)), S((2,)),
            S((16,)), S((16,)),
            S((1,)), S((1,)),
            S((15,)), S((15,)),
            S((10,)), S((10,)),
            S((1,)), S((1,)),
            S((2, 8, 2)), S((2, 8, 2)),
            S((2, 8)), S((2, 8)),
        ],
        compiler_params=pltpu.CompilerParams(
            collective_id=0, has_side_effects=True, vmem_limit_bytes=58 * 2**20
        ),
    )(
        tokens, queries, attn_keys, rt,
        w_in.reshape(16, 2, 256, 256), w_out, pick_rows.reshape(2, 16), counts.reshape(1, 2),
    )
    return pl.pallas_call(
        hand_over,
        name="hand_over",
        out_shape=(out, out),
        in_specs=[hbm, hbm],
        out_specs=(hbm, hbm),
        scratch_shapes=[V((4, 128, 512), BF), S((8,))],
    )(mixed, attended)


def solution(mesh):
    placed = (
        P("expert", "mp"),
        P("expert", "mp"),
        P("expert", "mp"),
        P("mp", None),
        P(None, ("expert", "mp")),
        P(("expert", "mp"), None),
        P(None, "expert", None),
        P(None, "expert"),
    )
    return jax.shard_map(
        body,
        mesh=mesh,
        in_specs=placed,
        out_specs=(P("expert", "mp"), P("expert", "mp")),
        check_vma=False,
    )
```

```python
import jax
import jax.numpy as jnp
from jax import lax
from jax.experimental import pallas as pl
from jax.experimental.pallas import tpu as pltpu
from jax.sharding import PartitionSpec as P

MESH = pl.DeviceIdType.MESH
HEAD_DIM = 128
BF = jnp.bfloat16
F32 = jnp.float32
NT = (((1,), (1,)), ((), ()))
INV_ROOT = HEAD_DIM ** (-0.5) * 1.4426950408889634
BLOCK_ROWS = 144


def dot(a, b):
    return jnp.dot(a, b, preferred_element_type=F32)


def dot_nt(a, b):
    return lax.dot_general(a, b, NT, preferred_element_type=F32)


def kernel(
    tok_h, qry_h, key_h, rt, win, wout, picks, cnts, mixed_o, att_o,
    tok, qry, key,
    a_msg, a_buf, xg, w1, w2, part, part_in, lgacc, hid, gate_s,
    outb, rs_in, t_sum, rp_in, f_sum, f_out, e_in, u_buf,
    kb, vb, acc, mrow, lrow, kp, wp, pos_col, pos_row,
    loc_sem, a_ss, a_rs, w_ss, w_rs, g_ss, g_rs, x_ss, x_rs,
    r_ss, r_rs, e_ss, e_rs, ep_ss, ep_rs, kv_ss, kv_rs, kvp_ss, kvp_rs,
):
    e = lax.axis_index("expert")
    m = lax.axis_index("mp")
    z, c = e // 2, lax.rem(e, 2)
    y, x = m // 4, lax.rem(m, 4)
    oc = 1 - c
    group = z // 4

    def dev(dz=0, dc=0, dy=0, dx=0):
        zz = lax.rem(z + dz + 8, 8)
        cc = lax.rem(c + dc, 2)
        return (zz * 2 + cc, lax.rem(y + dy + 4, 4) * 4 + lax.rem(x + dx + 4, 4))

    def along(i, j):
        return c * i + oc * j, oc * i + c * j

    def blk(i, j):
        dy, dx = along(i, j)
        return lax.rem(y + dy + 4, 4) * 4 + lax.rem(x + dx + 4, 4)

    def pdev(d):
        dy, dx = along(d, 0)
        return dev(dy=dy, dx=dx)

    def sdev(d):
        dy, dx = along(0, d)
        return dev(dy=dy, dx=dx)

    partner = dev(dc=1)
    sent = []

    def send(src, dst, ss, rs, to):
        cp = pltpu.make_async_remote_copy(
            src_ref=src, dst_ref=dst, send_sem=ss, recv_sem=rs, device_id=to, device_id_type=MESH
        )
        cp.start()
        sent.append(cp)
        return cp

    tok_in = pltpu.make_async_copy(tok_h, tok, loc_sem.at[2])
    key_in = pltpu.make_async_copy(key_h, key, loc_sem.at[3])
    qry_in = pltpu.make_async_copy(qry_h, qry, loc_sem.at[4])
    tok_in.start()
    key_in.start()
    qry_in.start()
    w1_loc = pltpu.make_async_copy(win.at[:, c], w1.at[c], loc_sem.at[0])
    w1_loc.start()
    barrier = pltpu.get_barrier_semaphore()
    for dz in range(8):
        for dc in range(2):
            if dz or dc:
                pl.semaphore_signal(barrier, inc=1, device_id=dev(dz, dc), device_id_type=MESH)
    for d in (1, 2, 3):
        pl.semaphore_signal(barrier, inc=1, device_id=dev(dy=d), device_id_type=MESH)
        pl.semaphore_signal(barrier, inc=1, device_id=dev(dx=d), device_id_type=MESH)

    row32 = lax.broadcasted_iota(jnp.int32, (32, 256), 0)
    lane32 = lax.broadcasted_iota(jnp.int32, (32, 256), 1)
    chosen = jnp.full((32, 256), -1, jnp.int32)
    row16 = lax.broadcasted_iota(jnp.int32, (16, 128), 0)
    lane16 = lax.broadcasted_iota(jnp.int32, (16, 128), 1)
    meta = jnp.where(row16 == 0, cnts[0, 0], jnp.where(row16 == 1, cnts[0, 1], 0))
    base = 16 * lax.rem(e, 8)
    for g in range(2):
        for j in range(16):
            pick = picks[g, j]
            live = jnp.where(j < cnts[0, g], pick, -1)
            chosen = jnp.where(row32 == 16 * g + j, live, chosen)
            meta = jnp.where(
                (row16 == 2 + 2 * g + e // 8) & (lane16 == base + j), pick, meta
            )
    onehot = jnp.where(chosen == lane32, 1.0, 0.0).astype(BF)
    tok_in.wait()
    rows = dot(onehot, tok[...]).astype(BF)
    meta_b = meta.astype(F32).astype(BF)
    for g in range(2):
        for h in range(2):
            a_msg[g, h, 0:16, :] = rows[16 * g : 16 * g + 16, 256 * h : 256 * h + 128]
            a_msg[g, h, 16:32, :] = rows[16 * g : 16 * g + 16, 256 * h + 128 : 256 * h + 256]
            a_msg[g, h, 32:48, :] = meta_b
    a_buf[e] = a_msg[group, c]
    pl.semaphore_wait(barrier, 21)

    a_cps = []
    for dz in (4, 3, 5, 2, 6, 1, 7, 0):
        for dc in range(2):
            if dz or dc:
                to_plane = lax.rem(z + dz, 8)
                to_core = lax.rem(c + dc, 2)
                a_cps.append(
                    send(
                        a_msg.at[to_plane // 4, to_core], a_buf.at[e],
                        a_ss.at[dz * 2 + dc], a_rs.at[dz * 2 + dc], dev(dz, dc),
                    )
                )

    def kv_send(buf, which, r_from, r_to, way, src=None):
        src = buf.at[r_from, c] if src is None else src
        return send(
            src, buf.at[r_to, c], kv_ss.at[which, r_to, way], kv_rs.at[which, r_to, way],
            dev(dz=1 if way == 0 else -1),
        )

    def kv_share(buf, which, r, src=None):
        src = buf.at[r, c] if src is None else src
        return send(src, buf.at[r, c], kvp_ss.at[which, r], kvp_rs.at[which, r], partner)

    key_in.wait()
    qry_in.wait()
    pieces = {}
    shared = {}
    pieces["k", 1] = kv_send(kb, 0, 0, 1, 0, key)
    pieces["v", 7] = kv_send(vb, 1, 0, 7, 1, tok)
    shared["k", 0] = kv_share(kb, 0, 0, key)
    shared["v", 0] = kv_share(vb, 1, 0, tok)
    pieces["v", 1] = kv_send(vb, 1, 0, 1, 0, tok)
    pieces["k", 7] = kv_send(kb, 0, 0, 7, 1, key)
    right = [("k", 1), ("v", 1), ("k", 2), ("v", 2), ("k", 3), ("v", 3), ("k", 4)]
    left = [("v", 7), ("k", 7), ("v", 6), ("k", 6), ("v", 5), ("k", 5), ("v", 4)]

    def pump(n):
        for way, (what, r) in ((0, right[n]), (1, left[n])):
            pieces[what, r].wait_recv()
            which, buf = (0, kb) if what == "k" else (1, vb)
            r_to = r + 1 if way == 0 else r - 1
            if (what, r_to) in (right if way == 0 else left):
                pieces[what, r_to] = kv_send(buf, which, r, r_to, way)
            shared[what, r] = kv_share(buf, which, r)

    w1_far = send(win.at[:, oc], w1.at[c], w_ss.at[0], w_rs.at[0], partner)

    def w2_copies():
        for b in range(16):
            mine = pl.ds(pl.multiple_of(512 * b + 256 * c, 256), 256)
            pltpu.make_async_copy(wout.at[:, mine], w2.at[c, b], loc_sem.at[1]).start()
        for b in range(16):
            other = pl.ds(pl.multiple_of(512 * b + 256 * oc, 256), 256)
            pltpu.make_async_remote_copy(
                src_ref=wout.at[:, other], dst_ref=w2.at[c, b], send_sem=w_ss.at[1],
                recv_sem=w_rs.at[1], device_id=partner, device_id_type=MESH,
            ).start()

    w2_copies()
    w2_loc = pltpu.make_async_copy(w2.at[c], w2.at[c], loc_sem.at[1])
    w2_far = pltpu.make_async_remote_copy(
        src_ref=w2.at[c], dst_ref=w2.at[c], send_sem=w_ss.at[1], recv_sem=w_rs.at[1],
        device_id=partner, device_id_type=MESH,
    )

    def soft_step(h, scores, v_h):
        hs = pl.ds(pl.multiple_of(h * 128, 128), 128)
        old = mrow[h][:, 0:1]
        new = jnp.maximum(old, jnp.max(scores, axis=1, keepdims=True))
        alpha = jnp.exp2((old - new) * INV_ROOT)
        w = jnp.exp2((scores - new) * INV_ROOT)
        total = w[:, 0:128]
        for i in range(1, scores.shape[1] // 128):
            total = total + w[:, 128 * i : 128 * i + 128]
        lrow[h] = lrow[h] * alpha + total
        acc[:, hs] = acc[:, hs] * alpha + dot(w.astype(BF), v_h)
        mrow[h] = jnp.broadcast_to(new, (256, 128))

    def attend_own():
        allowed = lax.broadcasted_iota(jnp.int32, (256, 256), 1) <= lax.broadcasted_iota(
            jnp.int32, (256, 256), 0
        )

        @pl.loop(0, 4)
        def _(h):
            hs = pl.ds(pl.multiple_of(h * 128, 128), 128)
            scores = jnp.where(allowed, dot_nt(qry[:, hs], key[:, hs]), -1e30)
            new = jnp.max(scores, axis=1, keepdims=True)
            w = jnp.exp2((scores - new) * INV_ROOT)
            lrow[h] = w[:, 0:128] + w[:, 128:256]
            acc[:, hs] = dot(w.astype(BF), tok[:, hs])
            mrow[h] = jnp.broadcast_to(new, (256, 128))

    def attend_partner():
        @pl.loop(0, 4)
        def _(h):
            hs = pl.ds(pl.multiple_of(h * 128, 128), 128)
            soft_step(h, dot_nt(qry[:, hs], kb[0, 0, :, hs]), vb[0, 0, :, hs])

    def attend_chip(r, first, last):
        @pl.loop(first, last)
        def _(h):
            hs = pl.ds(pl.multiple_of(h * 128, 128), 128)
            k_h = kb[r, :, :, hs].reshape(512, 128)
            v_h = vb[r, :, :, hs].reshape(512, 128)
            soft_step(h, dot_nt(qry[:, hs], k_h), v_h)

    def pick_keys(first, k_rows):
        n = k_rows.shape[0]
        at = lax.broadcasted_iota(jnp.int32, (256, n), 1) + first
        sel = jnp.where(pos_col[:, 0:1] == at, 1.0, 0.0).astype(BF)
        kp[...] += dot(sel, k_rows)

    def far_unit(d, side, part_no):
        r, ok = ((d, z >= d), (8 - d, z >= 8 - d))[side]
        if part_no == 0:
            for what in ("k", "v"):
                shared[what, r].wait_recv()

        @pl.when(ok)
        def _():
            if part_no < 2:
                attend_chip(r, 2 * part_no, 2 * part_no + 2)
            else:
                pick_keys((z - r) * 512, kb[r].reshape(512, 512))

    far = [(d, side, p) for d in (1, 2, 3) for side in (0, 1) for p in range(3)]

    def fill(n):
        for _ in range(n):
            if far:
                far_unit(*far.pop(0))

    attend_own()
    for what in ("k", "v"):
        shared[what, 0].wait_recv()

    @pl.when(c == 1)
    def _():
        attend_partner()

    for cp in a_cps:
        cp.wait_recv()
    lane_f = lane16.astype(F32)
    run = jnp.zeros((16, 128), F32)
    slot_at = [jnp.full((16, 128), -1.0, F32), jnp.full((16, 128), -1.0, F32)]
    picked_lane = jnp.zeros((16, 128), F32)
    for s in range(16):
        t = a_buf[s, 32:48, :].astype(F32)
        j = lane_f - 16.0 * (s % 8)
        here = (lane16 // 16 == s % 8) & (j < t)
        slot_at[s // 8] = jnp.where(here, run + j, slot_at[s // 8])
        run = run + t
        picked_lane = picked_lane + t
    row_f = lax.broadcasted_iota(jnp.int32, (128, 256), 0).astype(F32)
    row_l = lax.broadcasted_iota(jnp.int32, (16, 256), 0)
    lane_l = lax.broadcasted_iota(jnp.int32, (16, 256), 1)
    compact = []
    for g in range(2):
        at = jnp.concatenate([slot_at[0][g : g + 1], slot_at[1][g : g + 1]], axis=1)
        cmat = jnp.where(row_f == at, 1.0, 0.0).astype(BF)
        compact.append(cmat)
    mine = jnp.where(group == 0, compact[0].astype(F32), compact[1].astype(F32)).astype(BF)
    for h in range(2):
        got = a_buf[:, 16 * h : 16 * h + 16, :].reshape(256, 128)
        xg[m, 0:128, 128 * h : 128 * h + 128] = dot(mine, got).astype(BF)
    half_lanes = pl.ds(pl.multiple_of(256 * c, 256), 256)
    rt_row = jnp.where(group == 0, rt[0:1, half_lanes].astype(F32), rt[1:2, half_lanes].astype(F32))
    xg[m, 128:144, :] = jnp.broadcast_to(rt_row, (16, 256)).astype(BF)

    g_cps = {}

    def g_send(idx, b, to):
        g_cps[idx] = send(xg.at[b], xg.at[b], g_ss.at[idx], g_rs.at[idx], to)

    def g_second(i):
        for d in (2, 1, 3):
            g_send(3 + 3 * i + d, blk(i, 0), sdev(d))

    def g_wait(i, j):
        if j:
            g_cps[7 + 3 * i - j].wait_recv()
        elif i:
            g_cps[4 - i].wait_recv()

    for d in (2, 1, 3):
        g_send(d, m, pdev(d))
    g_second(0)

    at_lane = []
    for g in range(2):
        pk = jnp.concatenate(
            [picked_lane[2 + 2 * g : 3 + 2 * g], picked_lane[3 + 2 * g : 4 + 2 * g]], axis=1
        )
        info = jnp.where(
            row_l == 0, jnp.broadcast_to(pk, (16, 256)), (lane_l // 16).astype(F32)
        ).astype(BF)
        col = dot_nt(compact[g], info)
        pos_col[128 * g : 128 * g + 128, :] = jnp.broadcast_to(
            (col[:, 0:1] + 256.0 * col[:, 1:2]).astype(jnp.int32), (128, 128)
        )
        lane = dot_nt(info, compact[g])
        at_lane.append((lane[0:1] + 256.0 * lane[1:2]).astype(jnp.int32))
    pos_row[...] = jnp.broadcast_to(jnp.concatenate(at_lane, axis=1), (8, 256))
    kp[...] = jnp.zeros((256, 512), F32)
    pick_keys(e * 256, key[...])

    @pl.when(c == 1)
    def _():
        pick_keys(z * 512, kb[0, 0])

    part[...] = jnp.zeros((128, 640), F32)
    lgacc[...] = jnp.zeros((128, 16), F32)
    w1_loc.wait()
    w1_far.wait_recv()

    def mm1(i, j):
        b = blk(i, j)
        xb = xg[b, 0:128, :]
        part[:, 0:256] += dot(xb, w1[0, b])
        part[:, 256:512] += dot(xb, w1[1, b])
        lgacc[...] += dot_nt(xb, xg[b, 128:144, :])

    for i in (3, 1, 2):
        g_wait(i, 0)
        g_second(i)
    for i in (0, 3, 1, 2):
        mm1(i, 0)
    pump(0)
    for i in (0, 3, 1, 2):
        for j in (3, 1, 2):
            g_wait(i, j)
            mm1(i, j)
        if i == 3:
            pump(1)

    part[:, 512:640] = jnp.broadcast_to(lgacc[:, 0:1], (128, 128))
    x_cp = send(part, part_in, x_ss.at[0], x_rs.at[0], partner)
    fill(2)
    pump(2)
    fill(1)
    w2_loc.wait()
    w2_far.wait_recv()
    x_cp.wait_recv()
    hid[...] = jax.nn.gelu(part[:, 0:512] + part_in[:, 0:512]).astype(BF)
    gate_s[...] = jax.nn.sigmoid(part[:, 512:640] + part_in[:, 512:640])

    def mm2(i, j):
        b = blk(i, j)
        o = dot(hid[:, 0:256], w2[0, b]) + dot(hid[:, 256:512], w2[1, b])
        return o * gate_s[:, 0:1]

    r_cps = {}

    def r_send(idx, src, dst, to):
        r_cps[idx] = send(src, dst, r_ss.at[idx], r_rs.at[idx], to)

    for i in (2, 3, 1, 0):
        for j in (2, 3, 1):
            outb[i, j] = mm2(i, j).astype(BF)
            r_send(3 * i + j - 1, outb.at[i, j], rs_in.at[i, j - 1], sdev(j))
    pump(3)
    fill(3)

    def t_of(i):
        total = mm2(i, 0)
        for j in (3, 1, 2):
            r_cps[3 * i + j - 1].wait_recv()
            total = total + rs_in[i, j - 1].astype(F32)
        return total

    for i in (2, 3, 1):
        t_sum[i] = t_of(i).astype(BF)
        r_send(11 + i, t_sum.at[i], rp_in.at[i - 1], pdev(i))
    full = t_of(0)
    fill(4)
    for i in (3, 1, 2):
        r_cps[11 + i].wait_recv()
        full = full + rp_in[i - 1].astype(F32)
    f_sum[...] = full
    f_out[...] = full.astype(BF)

    zz = lax.rem(z, 4)
    e_cps = []
    for d in (2, 1, 3):
        to_q = lax.rem(zz + d, 4)
        e_cps.append(
            send(
                f_out.at[pl.ds(pl.multiple_of(32 * to_q, 32), 32)], e_in.at[d - 1],
                e_ss.at[d - 1], e_rs.at[d - 1], ((4 * group + to_q) * 2 + c, m),
            )
        )
    pump(4)
    fill(2)
    total = f_sum[pl.ds(pl.multiple_of(32 * zz, 32), 32), :]
    for cp in e_cps:
        cp.wait_recv()
    for d in range(3):
        total = total + e_in[d].astype(F32)
    my_rows = pl.ds(pl.multiple_of(32 * z, 32), 32)
    u_buf[c, my_rows, :] = total.astype(BF)
    u_cps = []
    for d in (4, 3, 5, 2, 6, 1, 7):
        u_cps.append(
            send(
                u_buf.at[c, my_rows], u_buf.at[c, my_rows], e_ss.at[2 + d], e_rs.at[2 + d], dev(dz=d)
            )
        )
    pump(5)
    fill(5)
    pump(6)
    fill(len(far))

    def attend_opposite(core):
        @pl.when(z >= 4)
        def _():
            @pl.loop(0, 4)
            def _(h):
                hs = pl.ds(pl.multiple_of(h * 128, 128), 128)
                soft_step(h, dot_nt(qry[:, hs], kb[4, core, :, hs]), vb[4, core, :, hs])

    for cp in u_cps:
        cp.wait_recv()
    u_share = send(u_buf.at[c], u_buf.at[c], ep_ss.at[0], ep_rs.at[0], partner)
    attend_opposite(c)
    shared["k", 4].wait_recv()
    shared["v", 4].wait_recv()
    attend_opposite(oc)

    @pl.when(z >= 4)
    def _():
        pick_keys((z - 4) * 512, kb[4].reshape(512, 512))


    seen = pos_row[0:1, :] <= lax.broadcasted_iota(jnp.int32, (256, 256), 0) + e * 256

    @pl.loop(0, 4)
    def _(h):
        hs = pl.ds(pl.multiple_of(h * 128, 128), 128)
        scores = dot_nt(qry[:, hs], kp[:, hs].astype(BF))
        w = jnp.exp2((scores - mrow[h][:, 0:1]) * INV_ROOT)
        wp[h] = jnp.where(seen, w, 0.0).astype(BF)

    u_share.wait_recv()

    hit = pos_row[0:1, :] == lax.broadcasted_iota(jnp.int32, (256, 256), 0) + e * 256
    scatter = jnp.where(hit, 1.0, 0.0).astype(BF)
    for h in range(2):
        cols = slice(256 * h, 256 * h + 256)
        mixed_o[:, cols] = (tok[:, cols].astype(F32) + dot(scatter, u_buf[h])).astype(BF)
    for h in range(4):
        cols = slice(128 * h, 128 * h + 128)
        u_h = u_buf[h // 2, :, 128 * (h % 2) : 128 * (h % 2) + 128]
        num = acc[:, cols] + dot(wp[h], u_h)
        den = jnp.sum(lrow[h], axis=1, keepdims=True)
        att_o[:, cols] = (num / den).astype(BF)

    for cp in sent:
        cp.wait_send()
    w2_far.wait_send()


def hand_over(mixed, attended, mixed_o, att_o, buf, sem):
    parts = [(a, b, i) for i in range(2) for a, b in ((mixed, mixed_o), (attended, att_o))]
    ins, outs = [], []
    for n, (a, b, i) in enumerate(parts):
        rows = pl.ds(128 * i, 128)
        ins.append(pltpu.make_async_copy(a.at[rows], buf.at[n], sem.at[n]))
        outs.append(pltpu.make_async_copy(buf.at[n], b.at[rows], sem.at[4 + n]))
    for cp in ins:
        cp.start()
    for i, cp in enumerate(ins):
        cp.wait()
        outs[i].start()
    for cp in outs:
        cp.wait()


def body(tokens, queries, attn_keys, router, w_in, w_out, pick_rows, counts):
    rt = router.T
    vm = pl.BlockSpec(memory_space=pltpu.VMEM)
    sm = pl.BlockSpec(memory_space=pltpu.SMEM)
    hbm = pl.BlockSpec(memory_space=pl.ANY)
    V = pltpu.VMEM
    S = pltpu.SemaphoreType.DMA
    out = jax.ShapeDtypeStruct((256, 512), BF)
    mixed, attended = pl.pallas_call(
        kernel,
        name="layer",
        out_shape=(out, out),
        in_specs=[hbm, hbm, hbm, vm, hbm, hbm, sm, sm],
        out_specs=(vm, vm),
        scratch_shapes=[
            V((256, 512), BF),
            V((256, 512), BF),
            V((256, 512), BF),
            V((2, 2, 48, 128), BF),
            V((16, 48, 128), BF),
            V((16, BLOCK_ROWS, 256), BF),
            V((2, 16, 256, 256), BF),
            V((2, 16, 256, 256), BF),
            V((128, 640), F32),
            V((128, 640), F32),
            V((128, 16), F32),
            V((128, 512), BF),
            V((128, 128), F32),
            V((4, 4, 128, 256), BF),
            V((4, 3, 128, 256), BF),
            V((4, 128, 256), BF),
            V((3, 128, 256), BF),
            V((128, 256), F32),
            V((128, 256), BF),
            V((3, 32, 256), BF),
            V((2, 256, 256), BF),
            V((8, 2, 256, 512), BF),
            V((8, 2, 256, 512), BF),
            V((256, 512), F32),
            V((4, 256, 128), F32),
            V((4, 256, 128), F32),
            V((256, 512), F32),
            V((4, 256, 256), BF),
            V((256, 128), jnp.int32),
            V((8, 256), jnp.int32),
            S((5,)),
            S((16,)), S((16,)),
            S((2,)), S((2,)),
            S((16,)), S((16,)),
            S((1,)), S((1,)),
            S((15,)), S((15,)),
            S((10,)), S((10,)),
            S((1,)), S((1,)),
            S((2, 8, 2)), S((2, 8, 2)),
            S((2, 8)), S((2, 8)),
        ],
        compiler_params=pltpu.CompilerParams(
            collective_id=0, has_side_effects=True, vmem_limit_bytes=58 * 2**20
        ),
    )(
        tokens, queries, attn_keys, rt,
        w_in.reshape(16, 2, 256, 256), w_out, pick_rows.reshape(2, 16), counts.reshape(1, 2),
    )
    return pl.pallas_call(
        hand_over,
        name="hand_over",
        out_shape=(out, out),
        in_specs=[hbm, hbm],
        out_specs=(hbm, hbm),
        scratch_shapes=[V((4, 128, 512), BF), S((8,))],
    )(mixed, attended)


def solution(mesh):
    placed = (
        P("expert", "mp"),
        P("expert", "mp"),
        P("expert", "mp"),
        P("mp", None),
        P(None, ("expert", "mp")),
        P(("expert", "mp"), None),
        P(None, "expert", None),
        P(None, "expert"),
    )
    return jax.shard_map(
        body,
        mesh=mesh,
        in_specs=placed,
        out_specs=(P("expert", "mp"), P("expert", "mp")),
        check_vma=False,
    )
```
